32 devices in a mesh: grp: 2 (over y), sp: 4 (over z), ch: 4 (over x, core).
Axes of the slice: x: 2, y: 2, z: 4, core: 2. Of those that a mesh axis runs over, the one named last changes fastest.
Arguments:
- state_field: bfloat16 [512, 768, 1440], P(('grp', 'ch'), 'sp'), parts along dimension 0, may hold values from -6 to 6
- spectral_weight: bfloat16 [2, 256, 256, 256], P(None, 'sp', 'ch'), may hold values from -0.5 to 0.5
- mode_gain: float32 [256, 320], P('ch'), may hold values from 0.5 to 2
- bypass_weight: bfloat16 [256, 256], replicated, may hold values from -0.375 to 0.375
Outputs:
- block_output: bfloat16 [512, 768, 1440], P(('grp', 'ch'), 'sp'), parts along dimension 0
The draws below stay inside these ranges and needn't reach their ends.
There are 2 independent parts, one for each index of `grp`. The reference program is written for one: setup_inputs(seed, part) draws one part's arguments, and reference() takes and returns one part's arrays. A program takes and returns all parts, laid end to end along the dimension named above; an argument that names none is the same for every part. Nothing has to cross between parts.
All inputs are finite; a program needn't handle non-finite values.
Results may differ from the reference program's by a relative error of at most 0.0069.
Values may be sent and summed in bfloat16 or wider, within the bound.
No kernel may reach another device: no remote copies, remote signals or barrier semaphores. Data moves between devices by JAX's collectives and lax.ppermute only.
A program may use at most 576 MiB of HBM per device.

```python
import math
import jax
import jax.numpy as jnp

C = 256
LAT = 768
LON = 1440
M = 256
L = 320


def strengthened(array, rng, source, target, shards_of, factor):
    def block_of(dim):
        return (jnp.arange(array.shape[dim]) // (array.shape[dim] // shards_of)).reshape((-1,) + (1,) * (array.ndim - 1 - dim))

    near = jax.random.permutation(rng, shards_of)[block_of(target)]
    far = (block_of(target) + shards_of // 2) % shards_of
    return jnp.where((block_of(source) == near) | (block_of(source) == far), factor * array, array)


def block_levels(own_key, dims, split, low, high):
    def one(position, blocks):
        heights = jax.random.uniform(jax.random.fold_in(jax.random.fold_in(own_key, 6), position), (blocks,), jnp.float32, low / len(split), high / len(split))
        return jnp.repeat(jnp.exp(heights), dims[position] // blocks).reshape((-1,) + (1,) * (len(dims) - position - 1))

    loudness = one(*split[0])
    for cut in split[1:]:
        loudness = loudness * one(*cut)
    return loudness


def noise(own_key, extent, spread, most, split=(), held_as=jnp.bfloat16):
    drawn = jax.random.normal(own_key, extent, jnp.float32) * spread
    if len(split) > 0:
        drawn = block_levels(own_key, extent, split, -0.22, 0.18) * drawn
    return jnp.clip(drawn, min=-most, max=most).astype(held_as)


def noise_with(key, extent, width, most, cuts, heavy, kind=jnp.bfloat16):
    array = width * jax.random.normal(key, extent, jnp.float32)
    if cuts:
        array = array * block_levels(key, extent, cuts, -0.22, 0.18)
    return jnp.clip(strengthened(array, jax.random.fold_in(key, 3), *heavy), -most, most).astype(kind)


def setup_inputs(seed: int = 0, part: int = 0) -> dict:
    keys = jax.random.split(jax.random.key(seed), 5)
    own_keys = jax.random.split(jax.random.fold_in(keys[4], part), 5)
    state_field = noise(own_keys[0], (C, LAT, LON), 1.0, 6.0, ((0, 4), (1, 4)))
    spectral_weight = noise_with(keys[1], (2, M, C, C), C ** -0.5, 0.5, ((1, 4), (2, 4)), (2, 3, 4, 2.0))
    mode_gain = jnp.clip(jnp.exp(math.log(2.0) - 1.3862944 * jax.random.uniform(keys[2], (C, L), jnp.float32) ** block_levels(keys[2], (C, L), ((0, 4),), -0.2, 0.2)), 0.5, 2.0)
    bypass_weight = noise(keys[3], (C, C), C ** -0.5, 0.375)
    return dict(state_field=state_field, spectral_weight=spectral_weight, mode_gain=mode_gain, bypass_weight=bypass_weight)


def make_tables():
    lon_index = jnp.arange(LON, dtype=jnp.int32)
    mode_index = jnp.arange(M, dtype=jnp.int32)
    phase_lon = jnp.mod(lon_index[:, None] * mode_index[None, :], LON).astype(jnp.float32) * (2.0 * math.pi / LON)
    fwd_lon = jnp.stack([jnp.cos(phase_lon), -jnp.sin(phase_lon)], axis=1).astype(jnp.bfloat16)
    mode_weight = jnp.where(mode_index == 0, 1.0, 2.0).astype(jnp.float32)
    inv_lon = jnp.stack([mode_weight[:, None] * jnp.cos(phase_lon).T, -mode_weight[:, None] * jnp.sin(phase_lon).T], axis=0).astype(jnp.bfloat16)
    lat_index = jnp.arange(LAT, dtype=jnp.int32)
    wave_index = jnp.arange(L, dtype=jnp.int32)
    wave_number = jnp.where(wave_index < L // 2, wave_index, wave_index - L).astype(jnp.int32)
    phase_lat = jnp.mod(lat_index[:, None] * wave_number[None, :], LAT).astype(jnp.float32) * (2.0 * math.pi / LAT)
    fwd_lat = jnp.stack([jnp.cos(phase_lat), jnp.sin(phase_lat)], axis=1).astype(jnp.bfloat16)
    inv_lat = jnp.stack([jnp.cos(phase_lat).T, jnp.sin(phase_lat).T], axis=1).astype(jnp.bfloat16)
    return fwd_lon, inv_lon, fwd_lat, inv_lat


def mix_modes(weights, inputs):
    weight_real = weights[0].astype(jnp.float32)
    weight_imag = weights[1].astype(jnp.float32)
    input_real = inputs[:, 0].astype(jnp.float32)
    input_imag = inputs[:, 1].astype(jnp.float32)
    out_real = jnp.einsum('mcd,cmk->dmk', weight_real, input_real) - jnp.einsum('mcd,cmk->dmk', weight_imag, input_imag)
    out_imag = jnp.einsum('mcd,cmk->dmk', weight_imag, input_real) + jnp.einsum('mcd,cmk->dmk', weight_real, input_imag)
    return jnp.stack([out_real, out_imag], axis=1)


def reference(state_field, spectral_weight, mode_gain, bypass_weight):
    fwd_lon, inv_lon, fwd_lat, inv_lat = make_tables()
    flat_field = state_field.reshape(C * LAT, LON)
    lon_spectrum = jnp.dot(flat_field, fwd_lon.reshape(LON, 2 * M), preferred_element_type=jnp.float32).astype(jnp.bfloat16).reshape(C, LAT, 2, M)
    lat_parts = jnp.einsum('clrm,lsk->crmsk', lon_spectrum.astype(jnp.float32), fwd_lat.astype(jnp.float32))
    real_part = lat_parts[:, 0, :, 0] + lat_parts[:, 1, :, 1]
    imag_part = lat_parts[:, 1, :, 0] - lat_parts[:, 0, :, 1]
    modes_in = jnp.stack([real_part, imag_part], axis=1).astype(jnp.bfloat16)
    mixed = mix_modes(spectral_weight, modes_in)
    scaled = (mixed * mode_gain[:, None, None, :]).astype(jnp.bfloat16)
    back_parts = jnp.einsum('drmk,ksl->drmsl', scaled.astype(jnp.float32), inv_lat.astype(jnp.float32))
    back_real = back_parts[:, 0, :, 0] - back_parts[:, 1, :, 1]
    back_imag = back_parts[:, 0, :, 1] + back_parts[:, 1, :, 0]
    lat_field = (jnp.stack([back_real, back_imag], axis=1) * (1.0 / LAT)).astype(jnp.bfloat16)
    spectral_out = jnp.einsum('drml,rmx->dlx', lat_field.astype(jnp.float32), inv_lon.astype(jnp.float32)) * (1.0 / LON)
    bypass = jnp.dot(bypass_weight.T, flat_field.reshape(C, LAT * LON), preferred_element_type=jnp.float32).astype(jnp.bfloat16).reshape(C, LAT, LON)
    return jax.nn.gelu(spectral_out + bypass.astype(jnp.float32), approximate=False).astype(jnp.bfloat16)
```

```python
import functools
import math

import jax
import jax.numpy as jnp
import ml_dtypes
import numpy as np
from jax import lax
from jax.experimental import pallas as pl
from jax.experimental.pallas import tpu as pltpu
from jax.sharding import PartitionSpec as P

LAT = 768
LON = 1440
M = 256
L = 320

LANES = 128
ROWS = 16
KPAD = 384
VMEM = 56 * 1024 * 1024
F32 = jnp.float32
BF16 = jnp.bfloat16


def make_tables():
    lon_index = jnp.arange(LON, dtype=jnp.int32)
    mode_index = jnp.arange(M, dtype=jnp.int32)
    phase_lon = jnp.mod(lon_index[:, None] * mode_index[None, :], LON).astype(jnp.float32) * (
        2.0 * math.pi / LON
    )
    fwd_lon = jnp.stack([jnp.cos(phase_lon), -jnp.sin(phase_lon)], axis=1).astype(jnp.bfloat16)
    mode_weight = jnp.where(mode_index == 0, 1.0, 2.0).astype(jnp.float32)
    inv_lon = jnp.stack(
        [mode_weight[:, None] * jnp.cos(phase_lon).T, -mode_weight[:, None] * jnp.sin(phase_lon).T],
        axis=0,
    ).astype(jnp.bfloat16)
    lat_index = jnp.arange(LAT, dtype=jnp.int32)
    wave_index = jnp.arange(L, dtype=jnp.int32)
    wave_number = jnp.where(wave_index < L // 2, wave_index, wave_index - L)
    phase_lat = jnp.mod(lat_index[:, None] * wave_number[None, :], LAT).astype(jnp.float32) * (
        2.0 * math.pi / LAT
    )
    fwd_lat = jnp.stack([jnp.cos(phase_lat), jnp.sin(phase_lat)], axis=1).astype(jnp.bfloat16)
    inv_lat = jnp.stack([jnp.cos(phase_lat).T, jnp.sin(phase_lat).T], axis=1).astype(jnp.bfloat16)
    return (fwd_lon, inv_lon, fwd_lat, inv_lat)


def mix_modes(weights, inputs):
    out_real = jnp.einsum(
        "mcd,cmk->dmk", weights[0], inputs[:, 0], preferred_element_type=jnp.float32
    ) - jnp.einsum("mcd,cmk->dmk", weights[1], inputs[:, 1], preferred_element_type=jnp.float32)
    out_imag = jnp.einsum(
        "mcd,cmk->dmk", weights[1], inputs[:, 0], preferred_element_type=jnp.float32
    ) + jnp.einsum("mcd,cmk->dmk", weights[0], inputs[:, 1], preferred_element_type=jnp.float32)
    return jnp.stack([out_real, out_imag], axis=1)


def plain_body(state_field, spectral_weight, mode_gain, bypass_weight):
    fwd_lon, inv_lon, fwd_lat, inv_lat = make_tables()
    chan_count = state_field.shape[0]
    band_rows = state_field.shape[1]
    flat_field = state_field.reshape(chan_count * band_rows, LON)
    lon_spectrum = (
        jnp.dot(flat_field, fwd_lon.reshape(LON, 2 * M), preferred_element_type=jnp.float32)
        .astype(jnp.bfloat16)
        .reshape(chan_count, band_rows, 2, M)
    )
    all_latitudes = lax.all_to_all(lon_spectrum, "sp", split_axis=3, concat_axis=1, tiled=True)
    lat_parts = jnp.einsum(
        "clrm,lsk->crmsk", all_latitudes, fwd_lat, preferred_element_type=jnp.float32
    )
    real_part = lat_parts[:, 0, :, 0] + lat_parts[:, 1, :, 1]
    imag_part = lat_parts[:, 1, :, 0] - lat_parts[:, 0, :, 1]
    modes_in = jnp.stack([real_part, imag_part], axis=1).astype(jnp.bfloat16)
    weight_rows = lax.all_to_all(spectral_weight, "ch", split_axis=3, concat_axis=2, tiled=True)
    all_inputs = lax.all_gather(modes_in, "ch", axis=0, tiled=True)
    mixed = mix_modes(weight_rows, all_inputs)
    scaled = (mixed * mode_gain[:, None, None, :]).astype(jnp.bfloat16)
    back_parts = jnp.einsum("drmk,ksl->drmsl", scaled, inv_lat, preferred_element_type=jnp.float32)
    back_real = back_parts[:, 0, :, 0] - back_parts[:, 1, :, 1]
    back_imag = back_parts[:, 0, :, 1] + back_parts[:, 1, :, 0]
    lat_field = (jnp.stack([back_real, back_imag], axis=1) * (1.0 / LAT)).astype(jnp.bfloat16)
    band_spectrum = lax.all_to_all(lat_field, "sp", split_axis=3, concat_axis=2, tiled=True)
    spectral_out = jnp.einsum(
        "drml,rmx->dlx", band_spectrum, inv_lon, preferred_element_type=jnp.float32
    ) * (1.0 / LON)
    out_width = bypass_weight.shape[1] // lax.axis_size("ch")
    own_columns = lax.dynamic_slice_in_dim(
        bypass_weight, lax.axis_index("ch") * out_width, out_width, 1
    )
    bypass = jnp.einsum(
        "cd,clx->dlx",
        own_columns,
        lax.all_gather(state_field, "ch", axis=0, tiled=True),
        preferred_element_type=jnp.float32,
    ).astype(jnp.bfloat16)
    return jax.nn.gelu(spectral_out + bypass.astype(jnp.float32), approximate=False).astype(
        jnp.bfloat16
    )


def lon_table(n_sp, modes, transposed):
    col = np.arange(n_sp * 2 * modes)
    imag, mode = (col // modes) % 2, col // (2 * modes) * modes + col % modes
    angle = (np.arange(LON)[:, None] * mode[None, :]) % LON * (2.0 * math.pi / LON)
    value = np.where(imag == 0, np.cos(angle), -np.sin(angle))
    if transposed:
        value = (value * np.where(mode == 0, 1.0, 2.0)).T
    return jnp.asarray(value.astype(ml_dtypes.bfloat16))


def lat_table():
    k = np.arange(L)
    kappa = np.where(k < L // 2, k, k - L)
    angle = (np.arange(LAT)[:, None] * kappa[None, :]) % LAT * (2.0 * math.pi / LAT)
    value = np.zeros((LAT, 2, KPAD))
    value[:, 0, :L], value[:, 1, :L] = np.cos(angle), np.sin(angle)
    return jnp.asarray(value.reshape(LAT, 2 * KPAD).astype(ml_dtypes.bfloat16))


MAP_COST = [0, 0, 120, 120, 80, 40]
FINISH_COST = [0, 0, 0, 0, 0, 0]


def call(kernel, name, cost=0, **kwargs):
    return pl.pallas_call(
        kernel,
        name=name,
        compiler_params=pltpu.CompilerParams(vmem_limit_bytes=VMEM),
        cost_estimate=pl.CostEstimate(
            flops=1 + int(cost * 1e9), bytes_accessed=1, transcendentals=0
        ),
        **kwargs,
    )


def const_spec(shape):
    return pl.BlockSpec(shape, lambda *_: (0,) * len(shape))


def kron_map(weight):
    c, d = weight.shape
    high, wide = d * ROWS, c * ROWS

    def kernel(w_ref, out):
        iota = functools.partial(lax.broadcasted_iota, jnp.int32)
        left = (iota((high, d), 0) // ROWS == iota((high, d), 1)).astype(F32).astype(BF16)
        right = (iota((c, wide), 1) // ROWS == iota((c, wide), 0)).astype(F32).astype(BF16)
        tall = lax.dot_general(
            left, w_ref[...], (((1,), (1,)), ((), ())), preferred_element_type=F32
        ).astype(BF16)
        value = jnp.dot(tall, right, preferred_element_type=F32)
        same = iota((high, wide), 0) % ROWS == iota((high, wide), 1) % ROWS
        out[...] = jnp.where(same, value, 0.0).astype(BF16)

    return call(
        kernel, "kron_map", out_shape=jax.ShapeDtypeStruct((high, wide), BF16)
    )(weight)


def pick_weights(ch, own, sibling):
    _, modes, chans, _ = own.shape
    half = LANES // 2
    step = modes // 4

    def kernel(ch_ref, a0, a1, b0, b1, out):
        for parity in range(2):

            @pl.when(ch_ref[0] % 2 == parity)
            def _():
                cols = slice(parity * half, (parity + 1) * half)
                for i, pair in enumerate(((a0, a1), (b0, b1))):
                    out[:, :, i * chans : (i + 1) * chans, :] = jnp.concatenate(
                        [ref[:, :, :, cols] for ref in pair], axis=-1
                    )

    def tile(far):
        return pl.BlockSpec(
            (2, step, chans, LANES), lambda i, ch_ref: (0, i, 0, (ch_ref[0] // 2 + far) % 2)
        )

    return call(
        kernel,
        "pick_weights",
        grid_spec=pltpu.PrefetchScalarGridSpec(
            num_scalar_prefetch=1,
            grid=(modes // step,),
            in_specs=[tile(0), tile(1), tile(0), tile(1)],
            out_specs=pl.BlockSpec((2, step, 2 * chans, LANES), lambda i, ch_ref: (0, i, 0, 0)),
        ),
        out_shape=jax.ShapeDtypeStruct((2, modes, 2 * chans, LANES), BF16),
    )(ch.reshape(1), own, own, sibling, sibling)


def lon_forward(field, table, start, count, n_sp):
    rows = field.shape[1]
    step = 4

    def kernel(s_ref, t_ref, out):
        s = s_ref[...].reshape(step * rows, LON)
        acc = jnp.dot(s, t_ref[...], preferred_element_type=F32)
        for k in range(n_sp):
            part = acc[:, k * LANES : (k + 1) * LANES].astype(BF16)
            out[k] = part.reshape(step, rows, LANES)

    return call(
        kernel,
        "lon_forward",
        grid=(count // step,),
        in_specs=[
            pl.BlockSpec((step, rows, LON), lambda i: (start // step + i, 0, 0)),
            const_spec(table.shape),
        ],
        out_specs=pl.BlockSpec((n_sp, step, rows, LANES), lambda i: (0, i, 0, 0)),
        out_shape=jax.ShapeDtypeStruct((n_sp, count, rows, LANES), BF16),
    )(field, table)


def lat_forward(bands, table):
    n_sp, count, rows, _ = bands.shape
    step = ROWS
    half = LANES // 2

    def kernel(x_ref, t_ref, out, left, right):
        for c in range(step):
            x = x_ref[:, c].reshape(n_sp * rows, LANES)
            left[c * LANES : (c + 1) * LANES, :] = x.T
        for c in range(step):
            g = jnp.dot(
                left[c * LANES : (c + 1) * LANES, :], t_ref[...], preferred_element_type=F32
            )
            right[c, :half, :] = g[:half, :KPAD] + g[half:, KPAD:]
            right[c, half:, :] = g[half:, :KPAD] - g[:half, KPAD:]
        out[...] = jnp.transpose(right[...], (1, 0, 2)).astype(BF16)

    return call(
        kernel,
        "lat_forward",
        grid=(count // step,),
        in_specs=[
            pl.BlockSpec((n_sp, step, rows, LANES), lambda i: (0, i, 0, 0)),
            const_spec(table.shape),
        ],
        out_specs=pl.BlockSpec((LANES, step, KPAD), lambda i: (0, i, 0)),
        out_shape=jax.ShapeDtypeStruct((LANES, count, KPAD), BF16),
        scratch_shapes=[
            pltpu.VMEM((step * LANES, n_sp * rows), BF16),
            pltpu.VMEM((step, LANES, KPAD), F32),
        ],
    )(bands, table)


def mix(weights, spectra, parts):
    modes, chans, outs2 = weights.shape[1:]
    outs = outs2 // 2
    step = ROWS
    n_in = len(spectra)

    def kernel(w_ref, *refs):
        ins, own, sends, scratch = refs[:n_in], refs[n_in], refs[n_in + 1 : -1], refs[-1]
        for m in range(step):
            y = jnp.concatenate([ref[r, m] for r in range(2) for ref in ins], axis=0)
            wr, wi = w_ref[0, m], w_ref[1, m]
            w = jnp.concatenate(
                [jnp.concatenate([wr, wi], axis=1), jnp.concatenate([-wi, wr], axis=1)], axis=0
            )
            scratch[m] = lax.dot_general(
                w, y, (((0,), (0,)), ((), ())), preferred_element_type=F32
            )
        for r in range(2):
            base = r * outs2
            own[r] = jnp.transpose(scratch[:, base : base + outs, :], (1, 0, 2))
        far = [
            jnp.transpose(scratch[:, r * outs2 + outs : (r + 1) * outs2, :], (1, 0, 2))
            for r in range(2)
        ]
        for i, send in enumerate(sends):
            block = [f[sum(parts[:i]) : sum(parts[: i + 1])] for f in far]
            for r in range(2):
                for t in range(2):
                    send[2 * r + t] = block[r][:, :, t * LANES : (t + 1) * LANES].astype(BF16)
            tail = [b[:, :, 2 * LANES : 2 * LANES + LANES // 2] for b in block]
            send[4] = jnp.concatenate(tail, axis=-1).astype(BF16)

    res = call(
        kernel,
        "mix",
        grid=(modes // step,),
        in_specs=[pl.BlockSpec((2, step, chans, outs2), lambda i: (0, i, 0, 0))]
        + [pl.BlockSpec((2, step, s.shape[2], KPAD), lambda i: (0, i, 0, 0)) for s in spectra],
        out_specs=[pl.BlockSpec((2, outs, step, KPAD), lambda i: (0, 0, i, 0))]
        + [pl.BlockSpec((5, per, step, LANES), lambda i: (0, 0, i, 0)) for per in parts],
        out_shape=[jax.ShapeDtypeStruct((2, outs, modes, KPAD), F32)]
        + [jax.ShapeDtypeStruct((5, per, modes, LANES), BF16) for per in parts],
        scratch_shapes=[pltpu.VMEM((step, 2 * outs2, KPAD), F32)],
    )(weights, *spectra)
    return res[0], res[1:]


def lat_backward(own, far, gain, table, start, n_sp):
    per, modes = far.shape[1:3]
    rows = LAT // n_sp
    step = 8

    def kernel(own_ref, far_ref, g_ref, t_ref, result):
        for pair in range(step // 2):
            blocks = []
            for d in (2 * pair, 2 * pair + 1):
                z = []
                for r in range(2):
                    tail = far_ref[4, d][:, r * (LANES // 2) : (r + 1) * (LANES // 2)]
                    sent = jnp.concatenate(
                        [
                            far_ref[2 * r, d].astype(F32),
                            far_ref[2 * r + 1, d].astype(F32),
                            tail.astype(F32),
                            jnp.zeros((modes, LANES // 2), F32),
                        ],
                        axis=-1,
                    )
                    z.append(((own_ref[r, d] + sent) * g_ref[d]).astype(BF16))
                blocks.append(jnp.concatenate([z[0], -z[1]], axis=1))
                blocks.append(jnp.concatenate([z[1], z[0]], axis=1))
            both = jnp.concatenate(blocks, axis=0)
            out = lax.dot_general(
                t_ref[...], both, (((1,), (1,)), ((), ())), preferred_element_type=F32
            ) * (1.0 / LAT)
            for k in range(n_sp):
                for i in range(2):
                    result[k, 2 * pair + i] = out[
                        k * rows : (k + 1) * rows, i * LANES : (i + 1) * LANES
                    ].astype(BF16)

    return call(
        kernel,
        "lat_backward",
        grid=(per // step,),
        in_specs=[
            pl.BlockSpec((2, step, modes, KPAD), lambda i: (0, start // step + i, 0, 0)),
            pl.BlockSpec((5, step, modes, LANES), lambda i: (0, i, 0, 0)),
            pl.BlockSpec((step, 1, KPAD), lambda i: (start // step + i, 0, 0)),
            const_spec(table.shape),
        ],
        out_specs=pl.BlockSpec((n_sp, step, rows, LANES), lambda i: (0, i, 0, 0)),
        out_shape=jax.ShapeDtypeStruct((n_sp, per, rows, LANES), BF16),
    )(own, far, gain, table)


WIDE = 2 * LANES
FULL = LON // WIDE
REST = LON - FULL * WIDE
TAIL = REST - LANES


def partial_map(field, sibling, kron, start, steps, cost):
    chans = field.shape[0]
    outs = kron.shape[0] // ROWS
    height = outs * ROWS
    depth = chans * ROWS
    packed = height * LON // LANES
    group = LANES // TAIL

    def kernel(a_ref, b_ref, w_ref, out):
        def product(cols, width):
            a = a_ref[:, :, cols].reshape(depth, width)
            b = b_ref[:, :, cols].reshape(depth, width)
            return jnp.dot(w_ref[:, :depth], a, preferred_element_type=F32) + jnp.dot(
                w_ref[:, depth:], b, preferred_element_type=F32
            )

        @pl.loop(0, FULL)
        def _(n):
            acc = product(pl.ds(pl.multiple_of(n * WIDE, WIDE), WIDE), WIDE).astype(BF16)
            base = pl.multiple_of(n * 2 * height, 2 * height)
            out[0, pl.ds(base, height), :] = acc[:, :LANES]
            out[0, pl.ds(base + height, height), :] = acc[:, LANES:]

        acc = product(slice(FULL * WIDE, LON), REST)
        out[0, FULL * 2 * height : (FULL * 2 + 1) * height, :] = acc[:, :LANES].astype(BF16)
        tail = acc[:, LANES:]
        size = height // group
        out[0, (FULL * 2 + 1) * height :, :] = jnp.concatenate(
            [tail[q * size : (q + 1) * size] for q in range(group)], axis=1
        ).astype(BF16)

    sib_start = start if sibling.shape[1] == field.shape[1] else 0
    return call(
        kernel,
        "partial_map",
        cost,
        grid=(steps,),
        in_specs=[
            pl.BlockSpec((chans, ROWS, LON), lambda i: (0, start + i, 0)),
            pl.BlockSpec((chans, ROWS, LON), lambda i: (0, sib_start + i, 0)),
            const_spec(kron.shape),
        ],
        out_specs=pl.BlockSpec((1, packed, LANES), lambda i: (i, 0, 0)),
        out_shape=jax.ShapeDtypeStruct((steps, packed, LANES), BF16),
    )(field, sibling, kron)


def gelu(v):
    return 0.5 * v * (1.0 + lax.erf(v * math.sqrt(0.5)))


def finish(previous, field, sibling, kron, spectrum, table, received, start, cost):
    chans = field.shape[0]
    outs = kron.shape[0] // ROWS
    height = outs * ROWS
    depth = chans * ROWS
    packed = height * LON // LANES
    group = LANES // TAIL
    n_sp = spectrum[0].shape[0]
    sizes = [part.shape[1] for part in spectrum]

    def kernel(*refs):
        refs = refs[1:] if previous is not None else refs
        a_ref, b_ref, w_ref, t_ref, p_ref = refs[:5]
        lats, out, lat = refs[5:-2], refs[-2], refs[-1]
        at = 0
        for ref, per in zip(lats, sizes):
            for k in range(n_sp):
                lat[at : at + per * ROWS, k * LANES : (k + 1) * LANES] = ref[k].reshape(
                    per * ROWS, LANES
                )
            at += per * ROWS

        def product(cols, width):
            a = a_ref[:, :, cols].reshape(depth, width)
            b = b_ref[:, :, cols].reshape(depth, width)
            spectral = jnp.dot(lat[...], t_ref[:, cols], preferred_element_type=F32)
            return (
                spectral * (1.0 / LON)
                + jnp.dot(w_ref[:, :depth], a, preferred_element_type=F32)
                + jnp.dot(w_ref[:, depth:], b, preferred_element_type=F32)
            )

        @pl.loop(0, FULL)
        def _(n):
            cols = pl.ds(pl.multiple_of(n * WIDE, WIDE), WIDE)
            acc = product(cols, WIDE)
            base = pl.multiple_of(n * 2 * height, 2 * height)
            far = jnp.concatenate(
                [p_ref[0, pl.ds(base, height), :], p_ref[0, pl.ds(base + height, height), :]], axis=1
            )
            value = gelu(acc + far.astype(F32)).astype(BF16)
            out[:, :, cols] = value.reshape(outs, ROWS, WIDE)

        acc = product(slice(FULL * WIDE, LON), REST)
        size = height // group
        tails = p_ref[0, (FULL * 2 + 1) * height :, :].astype(F32)
        tail = jnp.concatenate(
            [tails[:, q * TAIL : (q + 1) * TAIL] for q in range(group)], axis=0
        )
        far = p_ref[0, FULL * 2 * height : (FULL * 2 + 1) * height, :].astype(F32)
        one = gelu(acc[:, :LANES] + far).astype(BF16)
        out[:, :, FULL * WIDE : FULL * WIDE + LANES] = one.reshape(outs, ROWS, LANES)
        two = gelu(acc[:, LANES:] + tail).astype(BF16)
        out[:, :, FULL * WIDE + LANES :] = two.reshape(outs, ROWS, TAIL)

    steps = received.shape[0]
    operands = [field, sibling, kron, table, received, *spectrum]
    specs = [
        pl.BlockSpec((chans, ROWS, LON), lambda i: (0, start + i, 0)),
        pl.BlockSpec((chans, ROWS, LON), lambda i: (0, start + i, 0)),
        const_spec(kron.shape),
        const_spec(table.shape),
        pl.BlockSpec((1, packed, LANES), lambda i: (i, 0, 0)),
    ] + [
        pl.BlockSpec((n_sp, per, ROWS, LANES), lambda i: (0, 0, start + i, 0)) for per in sizes
    ]
    aliases = {}
    if previous is not None:
        operands = [previous] + operands
        specs = [pl.BlockSpec(memory_space=pl.ANY)] + specs
        aliases = {0: 0}
    return call(
        kernel,
        "finish",
        cost,
        grid=(steps,),
        in_specs=specs,
        out_specs=pl.BlockSpec((outs, ROWS, LON), lambda i: (0, start + i, 0)),
        out_shape=jax.ShapeDtypeStruct(field.shape, BF16),
        input_output_aliases=aliases,
        scratch_shapes=[pltpu.VMEM((height, n_sp * LANES), BF16)],
    )(*operands)


def after(value, *others):
    return lax.optimization_barrier((value, *others))[0]


def row_plan(total):
    unit = total // 12
    return [unit, 2 * unit, 3 * unit, 3 * unit, 2 * unit, total - 11 * unit]


def tiled_body(state_field, spectral_weight, mode_gain, bypass_weight):
    chans, rows, _ = state_field.shape
    modes = spectral_weight.shape[1]
    n_sp, n_ch = lax.axis_size("sp"), lax.axis_size("ch")
    ch = lax.axis_index("ch")
    near, far = jnp.bitwise_xor(ch, 1), jnp.bitwise_xor(ch, 2)

    def to_near(value):
        return lax.ppermute(value, "ch", [(i, i ^ 1) for i in range(n_ch)])

    def to_far(value):
        return lax.ppermute(value, "ch", [(i, i ^ 2) for i in range(n_ch)])

    def across(blocks):
        return lax.all_to_all(blocks, "sp", 0, 0)

    plan = row_plan(rows // ROWS)

    first = plan[0] * ROWS
    near_first = to_near(lax.slice_in_dim(state_field, 0, first, axis=1))
    near_field = to_near(after(state_field, near_first))
    near_weight = to_near(after(spectral_weight, near_first))

    def rows_of(index):
        return lax.dynamic_slice_in_dim(bypass_weight, index * chans, chans, 0)

    chip_rows = jnp.concatenate([rows_of(ch), rows_of(near)], axis=0)
    kron_far = kron_map(lax.dynamic_slice_in_dim(chip_rows, far * chans, chans, 1))
    kron_own = kron_map(lax.dynamic_slice_in_dim(chip_rows, ch * chans, chans, 1))

    sent, received, starts = [], [], []

    def partial_rows(*others):
        i = len(sent)
        starts.append(sum(plan[:i]))
        sibling = near_field if i else near_first
        kron = after(kron_far, *others)
        sent.append(partial_map(state_field, sibling, kron, starts[-1], plan[i], MAP_COST[i]))

    def send_rows(*others):
        received.append(to_far(after(sent[len(received)], *others)))

    half = chans // 2
    parts = [half, chans - half]
    table = lon_table(n_sp, modes, False)
    lat = lat_table()
    partial_rows()
    send_rows()
    table = after(table, sent[0])
    bands = [lon_forward(state_field, table, i * half, parts[i], n_sp) for i in range(2)]
    partial_rows(bands[0])
    send_rows(received[0])
    partial_rows(bands[1])
    send_rows(received[1])
    bands[1] = after(bands[1], sent[2])
    weights = pick_weights(ch, spectral_weight, near_weight)
    spectra = [lat_forward(across(b), lat).reshape(2, modes, -1, KPAD) for b in bands]
    near_spectra = [to_near(s) for s in spectra]

    own_mixed, sends = mix(weights, spectra + near_spectra, parts)
    far_mixed = [to_far(after(s, received[2])) for s in sends]

    gain = jnp.pad(mode_gain, ((0, 0), (0, KPAD - L))).reshape(chans, 1, KPAD)
    back = [lat_backward(own_mixed, far_mixed[i], gain, lat, i * half, n_sp) for i in range(2)]
    spectrum = [across(b) for b in back]
    partial_rows(*sends)
    send_rows(far_mixed[0])
    partial_rows(*sends)
    send_rows(received[3])
    partial_rows(*sends)
    send_rows(received[3])
    inverse = lon_table(n_sp, modes, True)
    out = None
    for got, start, cost in zip(received, starts, FINISH_COST):
        out = finish(
            out, state_field, near_field, kron_own, spectrum, inverse, got, start, cost
        )
    return out


def body(state_field, spectral_weight, mode_gain, bypass_weight):
    chans, rows, _ = state_field.shape
    modes = spectral_weight.shape[1]
    n_sp, n_ch = lax.axis_size("sp"), lax.axis_size("ch")
    whole_tiles = (
        n_ch == 4
        and 2 * modes == LANES
        and chans == 64
        and rows % (12 * ROWS) == 0
    )
    run = tiled_body if whole_tiles else plain_body
    return run(state_field, spectral_weight, mode_gain, bypass_weight)


def solution(mesh):
    in_specs = (P(("grp", "ch"), "sp", None), P(None, "sp", "ch", None), P("ch", None), P())
    out_specs = P(("grp", "ch"), "sp", None)
    return jax.shard_map(body, mesh=mesh, in_specs=in_specs, out_specs=out_specs, check_vma=False)
```

```python
import functools
import math

import jax
import jax.numpy as jnp
import ml_dtypes
import numpy as np
from jax import lax
from jax.experimental import pallas as pl
from jax.experimental.pallas import tpu as pltpu
from jax.sharding import PartitionSpec as P

LAT = 768
LON = 1440
M = 256
L = 320

LANES = 128
ROWS = 16
KPAD = 384
VMEM = 56 * 1024 * 1024
F32 = jnp.float32
BF16 = jnp.bfloat16


def make_tables():
    lon_index = jnp.arange(LON, dtype=jnp.int32)
    mode_index = jnp.arange(M, dtype=jnp.int32)
    phase_lon = jnp.mod(lon_index[:, None] * mode_index[None, :], LON).astype(jnp.float32) * (
        2.0 * math.pi / LON
    )
    fwd_lon = jnp.stack([jnp.cos(phase_lon), -jnp.sin(phase_lon)], axis=1).astype(jnp.bfloat16)
    mode_weight = jnp.where(mode_index == 0, 1.0, 2.0).astype(jnp.float32)
    inv_lon = jnp.stack(
        [mode_weight[:, None] * jnp.cos(phase_lon).T, -mode_weight[:, None] * jnp.sin(phase_lon).T],
        axis=0,
    ).astype(jnp.bfloat16)
    lat_index = jnp.arange(LAT, dtype=jnp.int32)
    wave_index = jnp.arange(L, dtype=jnp.int32)
    wave_number = jnp.where(wave_index < L // 2, wave_index, wave_index - L)
    phase_lat = jnp.mod(lat_index[:, None] * wave_number[None, :], LAT).astype(jnp.float32) * (
        2.0 * math.pi / LAT
    )
    fwd_lat = jnp.stack([jnp.cos(phase_lat), jnp.sin(phase_lat)], axis=1).astype(jnp.bfloat16)
    inv_lat = jnp.stack([jnp.cos(phase_lat).T, jnp.sin(phase_lat).T], axis=1).astype(jnp.bfloat16)
    return (fwd_lon, inv_lon, fwd_lat, inv_lat)


def mix_modes(weights, inputs):
    out_real = jnp.einsum(
        "mcd,cmk->dmk", weights[0], inputs[:, 0], preferred_element_type=jnp.float32
    ) - jnp.einsum("mcd,cmk->dmk", weights[1], inputs[:, 1], preferred_element_type=jnp.float32)
    out_imag = jnp.einsum(
        "mcd,cmk->dmk", weights[1], inputs[:, 0], preferred_element_type=jnp.float32
    ) + jnp.einsum("mcd,cmk->dmk", weights[0], inputs[:, 1], preferred_element_type=jnp.float32)
    return jnp.stack([out_real, out_imag], axis=1)


def plain_body(state_field, spectral_weight, mode_gain, bypass_weight):
    fwd_lon, inv_lon, fwd_lat, inv_lat = make_tables()
    chan_count = state_field.shape[0]
    band_rows = state_field.shape[1]
    flat_field = state_field.reshape(chan_count * band_rows, LON)
    lon_spectrum = (
        jnp.dot(flat_field, fwd_lon.reshape(LON, 2 * M), preferred_element_type=jnp.float32)
        .astype(jnp.bfloat16)
        .reshape(chan_count, band_rows, 2, M)
    )
    all_latitudes = lax.all_to_all(lon_spectrum, "sp", split_axis=3, concat_axis=1, tiled=True)
    lat_parts = jnp.einsum(
        "clrm,lsk->crmsk", all_latitudes, fwd_lat, preferred_element_type=jnp.float32
    )
    real_part = lat_parts[:, 0, :, 0] + lat_parts[:, 1, :, 1]
    imag_part = lat_parts[:, 1, :, 0] - lat_parts[:, 0, :, 1]
    modes_in = jnp.stack([real_part, imag_part], axis=1).astype(jnp.bfloat16)
    weight_rows = lax.all_to_all(spectral_weight, "ch", split_axis=3, concat_axis=2, tiled=True)
    all_inputs = lax.all_gather(modes_in, "ch", axis=0, tiled=True)
    mixed = mix_modes(weight_rows, all_inputs)
    scaled = (mixed * mode_gain[:, None, None, :]).astype(jnp.bfloat16)
    back_parts = jnp.einsum("drmk,ksl->drmsl", scaled, inv_lat, preferred_element_type=jnp.float32)
    back_real = back_parts[:, 0, :, 0] - back_parts[:, 1, :, 1]
    back_imag = back_parts[:, 0, :, 1] + back_parts[:, 1, :, 0]
    lat_field = (jnp.stack([back_real, back_imag], axis=1) * (1.0 / LAT)).astype(jnp.bfloat16)
    band_spectrum = lax.all_to_all(lat_field, "sp", split_axis=3, concat_axis=2, tiled=True)
    spectral_out = jnp.einsum(
        "drml,rmx->dlx", band_spectrum, inv_lon, preferred_element_type=jnp.float32
    ) * (1.0 / LON)
    out_width = bypass_weight.shape[1] // lax.axis_size("ch")
    own_columns = lax.dynamic_slice_in_dim(
        bypass_weight, lax.axis_index("ch") * out_width, out_width, 1
    )
    bypass = jnp.einsum(
        "cd,clx->dlx",
        own_columns,
        lax.all_gather(state_field, "ch", axis=0, tiled=True),
        preferred_element_type=jnp.float32,
    ).astype(jnp.bfloat16)
    return jax.nn.gelu(spectral_out + bypass.astype(jnp.float32), approximate=False).astype(
        jnp.bfloat16
    )


def lon_table(n_sp, modes, transposed):
    col = np.arange(n_sp * 2 * modes)
    imag, mode = (col // modes) % 2, col // (2 * modes) * modes + col % modes
    angle = (np.arange(LON)[:, None] * mode[None, :]) % LON * (2.0 * math.pi / LON)
    value = np.where(imag == 0, np.cos(angle), -np.sin(angle))
    if transposed:
        value = (value * np.where(mode == 0, 1.0, 2.0)).T
    return jnp.asarray(value.astype(ml_dtypes.bfloat16))


def lat_table():
    k = np.arange(L)
    kappa = np.where(k < L // 2, k, k - L)
    angle = (np.arange(LAT)[:, None] * kappa[None, :]) % LAT * (2.0 * math.pi / LAT)
    value = np.zeros((LAT, 2, KPAD))
    value[:, 0, :L], value[:, 1, :L] = np.cos(angle), np.sin(angle)
    return jnp.asarray(value.reshape(LAT, 2 * KPAD).astype(ml_dtypes.bfloat16))


MAP_COST = [0, 0, 120, 120, 80, 40]


def call(kernel, name, cost=0, **kwargs):
    return pl.pallas_call(
        kernel,
        name=name,
        compiler_params=pltpu.CompilerParams(vmem_limit_bytes=VMEM),
        cost_estimate=pl.CostEstimate(
            flops=1 + int(cost * 1e9), bytes_accessed=1, transcendentals=0
        ),
        **kwargs,
    )


def const_spec(shape):
    return pl.BlockSpec(shape, lambda *_: (0,) * len(shape))


def kron_map(weight):
    c, d = weight.shape
    high, wide = d * ROWS, c * ROWS

    def kernel(w_ref, out):
        iota = functools.partial(lax.broadcasted_iota, jnp.int32)
        left = (iota((high, d), 0) // ROWS == iota((high, d), 1)).astype(F32).astype(BF16)
        right = (iota((c, wide), 1) // ROWS == iota((c, wide), 0)).astype(F32).astype(BF16)
        tall = lax.dot_general(
            left, w_ref[...], (((1,), (1,)), ((), ())), preferred_element_type=F32
        ).astype(BF16)
        value = jnp.dot(tall, right, preferred_element_type=F32)
        same = iota((high, wide), 0) % ROWS == iota((high, wide), 1) % ROWS
        out[...] = jnp.where(same, value, 0.0).astype(BF16)

    return call(
        kernel, "kron_map", out_shape=jax.ShapeDtypeStruct((high, wide), BF16)
    )(weight)


def pick_weights(ch, own, sibling):
    _, modes, chans, _ = own.shape
    half = LANES // 2
    step = modes // 4

    def kernel(ch_ref, a0, a1, b0, b1, out):
        for parity in range(2):

            @pl.when(ch_ref[0] % 2 == parity)
            def _():
                cols = slice(parity * half, (parity + 1) * half)
                for i, pair in enumerate(((a0, a1), (b0, b1))):
                    out[:, :, i * chans : (i + 1) * chans, :] = jnp.concatenate(
                        [ref[:, :, :, cols] for ref in pair], axis=-1
                    )

    def tile(far):
        return pl.BlockSpec(
            (2, step, chans, LANES), lambda i, ch_ref: (0, i, 0, (ch_ref[0] // 2 + far) % 2)
        )

    return call(
        kernel,
        "pick_weights",
        grid_spec=pltpu.PrefetchScalarGridSpec(
            num_scalar_prefetch=1,
            grid=(modes // step,),
            in_specs=[tile(0), tile(1), tile(0), tile(1)],
            out_specs=pl.BlockSpec((2, step, 2 * chans, LANES), lambda i, ch_ref: (0, i, 0, 0)),
        ),
        out_shape=jax.ShapeDtypeStruct((2, modes, 2 * chans, LANES), BF16),
    )(ch.reshape(1), own, own, sibling, sibling)


def lon_forward(field, table, start, count, n_sp):
    rows = field.shape[1]
    step = 4

    def kernel(s_ref, t_ref, out):
        s = s_ref[...].reshape(step * rows, LON)
        acc = jnp.dot(s, t_ref[...], preferred_element_type=F32)
        for k in range(n_sp):
            part = acc[:, k * LANES : (k + 1) * LANES].astype(BF16)
            out[k] = part.reshape(step, rows, LANES)

    return call(
        kernel,
        "lon_forward",
        grid=(count // step,),
        in_specs=[
            pl.BlockSpec((step, rows, LON), lambda i: (start // step + i, 0, 0)),
            const_spec(table.shape),
        ],
        out_specs=pl.BlockSpec((n_sp, step, rows, LANES), lambda i: (0, i, 0, 0)),
        out_shape=jax.ShapeDtypeStruct((n_sp, count, rows, LANES), BF16),
    )(field, table)


def lat_forward(bands, table):
    n_sp, count, rows, _ = bands.shape
    step = ROWS
    half = LANES // 2

    def kernel(x_ref, t_ref, out, left, right):
        for c in range(step):
            x = x_ref[:, c].reshape(n_sp * rows, LANES)
            left[c * LANES : (c + 1) * LANES, :] = x.T
        for c in range(step):
            g = jnp.dot(
                left[c * LANES : (c + 1) * LANES, :], t_ref[...], preferred_element_type=F32
            )
            right[c, :half, :] = g[:half, :KPAD] + g[half:, KPAD:]
            right[c, half:, :] = g[half:, :KPAD] - g[:half, KPAD:]
        out[...] = jnp.transpose(right[...], (1, 0, 2)).astype(BF16)

    return call(
        kernel,
        "lat_forward",
        grid=(count // step,),
        in_specs=[
            pl.BlockSpec((n_sp, step, rows, LANES), lambda i: (0, i, 0, 0)),
            const_spec(table.shape),
        ],
        out_specs=pl.BlockSpec((LANES, step, KPAD), lambda i: (0, i, 0)),
        out_shape=jax.ShapeDtypeStruct((LANES, count, KPAD), BF16),
        scratch_shapes=[
            pltpu.VMEM((step * LANES, n_sp * rows), BF16),
            pltpu.VMEM((step, LANES, KPAD), F32),
        ],
    )(bands, table)


def mix(weights, spectra, parts):
    modes, chans, outs2 = weights.shape[1:]
    outs = outs2 // 2
    step = ROWS
    n_in = len(spectra)

    def kernel(w_ref, *refs):
        ins, own, sends, scratch = refs[:n_in], refs[n_in], refs[n_in + 1 : -1], refs[-1]
        for m in range(step):
            y = jnp.concatenate([ref[r, m] for r in range(2) for ref in ins], axis=0)
            wr, wi = w_ref[0, m], w_ref[1, m]
            w = jnp.concatenate(
                [jnp.concatenate([wr, wi], axis=1), jnp.concatenate([-wi, wr], axis=1)], axis=0
            )
            scratch[m] = lax.dot_general(
                w, y, (((0,), (0,)), ((), ())), preferred_element_type=F32
            )
        for r in range(2):
            base = r * outs2
            own[r] = jnp.transpose(scratch[:, base : base + outs, :], (1, 0, 2))
        far = [
            jnp.transpose(scratch[:, r * outs2 + outs : (r + 1) * outs2, :], (1, 0, 2))
            for r in range(2)
        ]
        for i, send in enumerate(sends):
            block = [f[sum(parts[:i]) : sum(parts[: i + 1])] for f in far]
            for r in range(2):
                for t in range(2):
                    send[2 * r + t] = block[r][:, :, t * LANES : (t + 1) * LANES].astype(BF16)
            tail = [b[:, :, 2 * LANES : 2 * LANES + LANES // 2] for b in block]
            send[4] = jnp.concatenate(tail, axis=-1).astype(BF16)

    res = call(
        kernel,
        "mix",
        grid=(modes // step,),
        in_specs=[pl.BlockSpec((2, step, chans, outs2), lambda i: (0, i, 0, 0))]
        + [pl.BlockSpec((2, step, s.shape[2], KPAD), lambda i: (0, i, 0, 0)) for s in spectra],
        out_specs=[pl.BlockSpec((2, outs, step, KPAD), lambda i: (0, 0, i, 0))]
        + [pl.BlockSpec((5, per, step, LANES), lambda i: (0, 0, i, 0)) for per in parts],
        out_shape=[jax.ShapeDtypeStruct((2, outs, modes, KPAD), F32)]
        + [jax.ShapeDtypeStruct((5, per, modes, LANES), BF16) for per in parts],
        scratch_shapes=[pltpu.VMEM((step, 2 * outs2, KPAD), F32)],
    )(weights, *spectra)
    return res[0], res[1:]


def lat_backward(own, far, gain, table, start, n_sp):
    per, modes = far.shape[1:3]
    rows = LAT // n_sp
    step = 8

    def kernel(own_ref, far_ref, g_ref, t_ref, result):
        for pair in range(step // 2):
            blocks = []
            for d in (2 * pair, 2 * pair + 1):
                z = []
                for r in range(2):
                    tail = far_ref[4, d][:, r * (LANES // 2) : (r + 1) * (LANES // 2)]
                    sent = jnp.concatenate(
                        [
                            far_ref[2 * r, d].astype(F32),
                            far_ref[2 * r + 1, d].astype(F32),
                            tail.astype(F32),
                            jnp.zeros((modes, LANES // 2), F32),
                        ],
                        axis=-1,
                    )
                    z.append(((own_ref[r, d] + sent) * g_ref[d]).astype(BF16))
                blocks.append(jnp.concatenate([z[0], -z[1]], axis=1))
                blocks.append(jnp.concatenate([z[1], z[0]], axis=1))
            both = jnp.concatenate(blocks, axis=0)
            out = lax.dot_general(
                t_ref[...], both, (((1,), (1,)), ((), ())), preferred_element_type=F32
            ) * (1.0 / LAT)
            for k in range(n_sp):
                for i in range(2):
                    result[k, 2 * pair + i] = out[
                        k * rows : (k + 1) * rows, i * LANES : (i + 1) * LANES
                    ].astype(BF16)

    return call(
        kernel,
        "lat_backward",
        grid=(per // step,),
        in_specs=[
            pl.BlockSpec((2, step, modes, KPAD), lambda i: (0, start // step + i, 0, 0)),
            pl.BlockSpec((5, step, modes, LANES), lambda i: (0, i, 0, 0)),
            pl.BlockSpec((step, 1, KPAD), lambda i: (start // step + i, 0, 0)),
            const_spec(table.shape),
        ],
        out_specs=pl.BlockSpec((n_sp, step, rows, LANES), lambda i: (0, i, 0, 0)),
        out_shape=jax.ShapeDtypeStruct((n_sp, per, rows, LANES), BF16),
    )(own, far, gain, table)


WIDE = 2 * LANES
FULL = LON // WIDE
REST = LON - FULL * WIDE
TAIL = REST - LANES


def partial_map(field, sibling, kron, start, steps, cost):
    chans = field.shape[0]
    outs = kron.shape[0] // ROWS
    height = outs * ROWS
    depth = chans * ROWS
    packed = height * LON // LANES
    group = LANES // TAIL

    def kernel(a_ref, b_ref, w_ref, out):
        def product(cols, width):
            a = a_ref[:, :, cols].reshape(depth, width)
            b = b_ref[:, :, cols].reshape(depth, width)
            return jnp.dot(w_ref[:, :depth], a, preferred_element_type=F32) + jnp.dot(
                w_ref[:, depth:], b, preferred_element_type=F32
            )

        @pl.loop(0, FULL)
        def _(n):
            acc = product(pl.ds(pl.multiple_of(n * WIDE, WIDE), WIDE), WIDE).astype(BF16)
            base = pl.multiple_of(n * 2 * height, 2 * height)
            out[0, pl.ds(base, height), :] = acc[:, :LANES]
            out[0, pl.ds(base + height, height), :] = acc[:, LANES:]

        acc = product(slice(FULL * WIDE, LON), REST)
        out[0, FULL * 2 * height : (FULL * 2 + 1) * height, :] = acc[:, :LANES].astype(BF16)
        tail = acc[:, LANES:]
        size = height // group
        out[0, (FULL * 2 + 1) * height :, :] = jnp.concatenate(
            [tail[q * size : (q + 1) * size] for q in range(group)], axis=1
        ).astype(BF16)

    sib_start = start if sibling.shape[1] == field.shape[1] else 0
    return call(
        kernel,
        "partial_map",
        cost,
        grid=(steps,),
        in_specs=[
            pl.BlockSpec((chans, ROWS, LON), lambda i: (0, start + i, 0)),
            pl.BlockSpec((chans, ROWS, LON), lambda i: (0, sib_start + i, 0)),
            const_spec(kron.shape),
        ],
        out_specs=pl.BlockSpec((1, packed, LANES), lambda i: (i, 0, 0)),
        out_shape=jax.ShapeDtypeStruct((steps, packed, LANES), BF16),
    )(field, sibling, kron)


def own_map(field, sibling, kron, start, steps):
    chans = field.shape[0]
    outs = kron.shape[0] // ROWS
    depth = chans * ROWS

    def kernel(a_ref, b_ref, w_ref, out):
        def product(cols, width):
            a = a_ref[:, :, cols].reshape(depth, width)
            b = b_ref[:, :, cols].reshape(depth, width)
            acc = jnp.dot(w_ref[:, :depth], a, preferred_element_type=F32) + jnp.dot(
                w_ref[:, depth:], b, preferred_element_type=F32
            )
            out[:, :, cols] = acc.reshape(outs, ROWS, width)

        @pl.loop(0, FULL)
        def _(n):
            product(pl.ds(pl.multiple_of(n * WIDE, WIDE), WIDE), WIDE)

        product(slice(FULL * WIDE, LON), REST)

    rows = pl.BlockSpec((chans, ROWS, LON), lambda i: (0, start + i, 0))
    return call(
        kernel,
        "own_map",
        grid=(steps,),
        in_specs=[rows, rows, const_spec(kron.shape)],
        out_specs=pl.BlockSpec((outs, ROWS, LON), lambda i: (0, i, 0)),
        out_shape=jax.ShapeDtypeStruct((outs, steps * ROWS, LON), F32),
    )(field, sibling, kron)


def gelu(v):
    return 0.5 * v * (1.0 + lax.erf(v * math.sqrt(0.5)))


def finish(previous, own, spectrum, table, received, start, own_start, shape, cost):
    outs = own.shape[0]
    height = outs * ROWS
    packed = height * LON // LANES
    group = LANES // TAIL
    n_sp = spectrum[0].shape[0]
    sizes = [part.shape[1] for part in spectrum]

    def kernel(*refs):
        refs = refs[1:] if previous is not None else refs
        o_ref, t_ref, p_ref = refs[:3]
        lats, out, lat = refs[3:-2], refs[-2], refs[-1]
        at = 0
        for ref, per in zip(lats, sizes):
            for k in range(n_sp):
                lat[at : at + per * ROWS, k * LANES : (k + 1) * LANES] = ref[k].reshape(
                    per * ROWS, LANES
                )
            at += per * ROWS

        def product(cols, width):
            spectral = jnp.dot(lat[...], t_ref[:, cols], preferred_element_type=F32)
            return spectral * (1.0 / LON) + o_ref[:, :, cols].reshape(height, width)

        @pl.loop(0, FULL)
        def _(n):
            cols = pl.ds(pl.multiple_of(n * WIDE, WIDE), WIDE)
            acc = product(cols, WIDE)
            base = pl.multiple_of(n * 2 * height, 2 * height)
            far = jnp.concatenate(
                [p_ref[0, pl.ds(base, height), :], p_ref[0, pl.ds(base + height, height), :]], axis=1
            )
            value = gelu(acc + far.astype(F32)).astype(BF16)
            out[:, :, cols] = value.reshape(outs, ROWS, WIDE)

        acc = product(slice(FULL * WIDE, LON), REST)
        size = height // group
        tails = p_ref[0, (FULL * 2 + 1) * height :, :].astype(F32)
        tail = jnp.concatenate(
            [tails[:, q * TAIL : (q + 1) * TAIL] for q in range(group)], axis=0
        )
        far = p_ref[0, FULL * 2 * height : (FULL * 2 + 1) * height, :].astype(F32)
        one = gelu(acc[:, :LANES] + far).astype(BF16)
        out[:, :, FULL * WIDE : FULL * WIDE + LANES] = one.reshape(outs, ROWS, LANES)
        two = gelu(acc[:, LANES:] + tail).astype(BF16)
        out[:, :, FULL * WIDE + LANES :] = two.reshape(outs, ROWS, TAIL)

    steps = received.shape[0]
    operands = [own, table, received, *spectrum]
    specs = [
        pl.BlockSpec((outs, ROWS, LON), lambda i: (0, own_start + i, 0)),
        const_spec(table.shape),
        pl.BlockSpec((1, packed, LANES), lambda i: (i, 0, 0)),
    ] + [
        pl.BlockSpec((n_sp, per, ROWS, LANES), lambda i: (0, 0, start + i, 0)) for per in sizes
    ]
    aliases = {}
    if previous is not None:
        operands = [previous] + operands
        specs = [pl.BlockSpec(memory_space=pl.ANY)] + specs
        aliases = {0: 0}
    return call(
        kernel,
        "finish",
        cost,
        grid=(steps,),
        in_specs=specs,
        out_specs=pl.BlockSpec((outs, ROWS, LON), lambda i: (0, start + i, 0)),
        out_shape=jax.ShapeDtypeStruct(shape, BF16),
        input_output_aliases=aliases,
        scratch_shapes=[pltpu.VMEM((height, n_sp * LANES), BF16)],
    )(*operands)


def after(value, *others):
    return lax.optimization_barrier((value, *others))[0]


def row_plan(total):
    unit = total // 12
    return [unit, 2 * unit, 3 * unit, 3 * unit, 2 * unit, total - 11 * unit]


def tiled_body(state_field, spectral_weight, mode_gain, bypass_weight):
    chans, rows, _ = state_field.shape
    modes = spectral_weight.shape[1]
    n_sp, n_ch = lax.axis_size("sp"), lax.axis_size("ch")
    ch = lax.axis_index("ch")
    near, far = jnp.bitwise_xor(ch, 1), jnp.bitwise_xor(ch, 2)

    def to_near(value):
        return lax.ppermute(value, "ch", [(i, i ^ 1) for i in range(n_ch)])

    def to_far(value):
        return lax.ppermute(value, "ch", [(i, i ^ 2) for i in range(n_ch)])

    def across(blocks):
        return lax.all_to_all(blocks, "sp", 0, 0)

    plan = row_plan(rows // ROWS)

    first = plan[0] * ROWS
    near_first = to_near(lax.slice_in_dim(state_field, 0, first, axis=1))
    def rows_of(index):
        return lax.dynamic_slice_in_dim(bypass_weight, index * chans, chans, 0)

    chip_rows = jnp.concatenate([rows_of(ch), rows_of(near)], axis=0)
    kron_far = kron_map(lax.dynamic_slice_in_dim(chip_rows, far * chans, chans, 1))
    kron_own = kron_map(lax.dynamic_slice_in_dim(chip_rows, ch * chans, chans, 1))

    near_field = to_near(after(state_field, near_first, kron_far))
    near_weight = to_near(after(spectral_weight, near_first))

    sent, received, starts = [], [], []

    def partial_rows(*others):
        i = len(sent)
        starts.append(sum(plan[:i]))
        sibling = near_field if i else near_first
        kron = after(kron_far, *others)
        sent.append(partial_map(state_field, sibling, kron, starts[-1], plan[i], MAP_COST[i]))

    def send_rows(*others):
        received.append(to_far(after(sent[len(received)], *others)))

    half = chans // 2
    parts = [half, chans - half]
    table = lon_table(n_sp, modes, False)
    lat = lat_table()
    partial_rows()
    send_rows()
    table = after(table, sent[0])
    bands = [lon_forward(state_field, table, i * half, parts[i], n_sp) for i in range(2)]
    partial_rows(bands[0])
    send_rows(received[0])
    partial_rows(bands[1])
    send_rows(received[1])
    middle = sum(plan[:3])
    own = [own_map(state_field, near_field, after(kron_own, sent[2]), 0, middle)]
    bands[1] = after(bands[1], sent[2], own[0])
    weights = pick_weights(ch, spectral_weight, near_weight)
    bands = [across(b) for b in bands]
    spectra = [lat_forward(bands[0], lat)]
    own.append(own_map(state_field, near_field, after(kron_own, spectra[0]), middle, sum(plan[3:])))
    spectra.append(lat_forward(bands[1], after(lat, own[1])))
    spectra = [s.reshape(2, modes, -1, KPAD) for s in spectra]
    near_spectra = [to_near(s) for s in spectra]

    own_mixed, sends = mix(weights, spectra + near_spectra, parts)
    far_mixed = [to_far(after(s, received[2])) for s in sends]

    gain = jnp.pad(mode_gain, ((0, 0), (0, KPAD - L))).reshape(chans, 1, KPAD)
    back = [lat_backward(own_mixed, far_mixed[i], gain, lat, i * half, n_sp) for i in range(2)]
    spectrum = [across(b) for b in back]
    partial_rows(*sends)
    send_rows(far_mixed[0])
    partial_rows(*sends)
    send_rows(received[3])
    partial_rows(*sends)
    send_rows(received[3])
    inverse = lon_table(n_sp, modes, True)
    out = None
    for got, start in zip(received, starts):
        late = start >= middle
        out = finish(
            out, own[late], spectrum, inverse, got, start, start - late * middle, state_field.shape, 0
        )
    return out


def body(state_field, spectral_weight, mode_gain, bypass_weight):
    chans, rows, _ = state_field.shape
    modes = spectral_weight.shape[1]
    n_sp, n_ch = lax.axis_size("sp"), lax.axis_size("ch")
    whole_tiles = (
        n_ch == 4
        and 2 * modes == LANES
        and chans == 64
        and rows % (12 * ROWS) == 0
    )
    run = tiled_body if whole_tiles else plain_body
    return run(state_field, spectral_weight, mode_gain, bypass_weight)


def solution(mesh):
    in_specs = (P(("grp", "ch"), "sp", None), P(None, "sp", "ch", None), P("ch", None), P())
    out_specs = P(("grp", "ch"), "sp", None)
    return jax.shard_map(body, mesh=mesh, in_specs=in_specs, out_specs=out_specs, check_vma=False)
```

```python
import functools
import math

import jax
import jax.numpy as jnp
import ml_dtypes
import numpy as np
from jax import lax
from jax.experimental import pallas as pl
from jax.experimental.pallas import tpu as pltpu
from jax.sharding import PartitionSpec as P

LAT = 768
LON = 1440
M = 256
L = 320

LANES = 128
ROWS = 16
KPAD = 384
VMEM = 56 * 1024 * 1024
F32 = jnp.float32
BF16 = jnp.bfloat16


def make_tables():
    lon_index = jnp.arange(LON, dtype=jnp.int32)
    mode_index = jnp.arange(M, dtype=jnp.int32)
    phase_lon = jnp.mod(lon_index[:, None] * mode_index[None, :], LON).astype(jnp.float32) * (
        2.0 * math.pi / LON
    )
    fwd_lon = jnp.stack([jnp.cos(phase_lon), -jnp.sin(phase_lon)], axis=1).astype(jnp.bfloat16)
    mode_weight = jnp.where(mode_index == 0, 1.0, 2.0).astype(jnp.float32)
    inv_lon = jnp.stack(
        [mode_weight[:, None] * jnp.cos(phase_lon).T, -mode_weight[:, None] * jnp.sin(phase_lon).T],
        axis=0,
    ).astype(jnp.bfloat16)
    lat_index = jnp.arange(LAT, dtype=jnp.int32)
    wave_index = jnp.arange(L, dtype=jnp.int32)
    wave_number = jnp.where(wave_index < L // 2, wave_index, wave_index - L)
    phase_lat = jnp.mod(lat_index[:, None] * wave_number[None, :], LAT).astype(jnp.float32) * (
        2.0 * math.pi / LAT
    )
    fwd_lat = jnp.stack([jnp.cos(phase_lat), jnp.sin(phase_lat)], axis=1).astype(jnp.bfloat16)
    inv_lat = jnp.stack([jnp.cos(phase_lat).T, jnp.sin(phase_lat).T], axis=1).astype(jnp.bfloat16)
    return (fwd_lon, inv_lon, fwd_lat, inv_lat)


def mix_modes(weights, inputs):
    out_real = jnp.einsum(
        "mcd,cmk->dmk", weights[0], inputs[:, 0], preferred_element_type=jnp.float32
    ) - jnp.einsum("mcd,cmk->dmk", weights[1], inputs[:, 1], preferred_element_type=jnp.float32)
    out_imag = jnp.einsum(
        "mcd,cmk->dmk", weights[1], inputs[:, 0], preferred_element_type=jnp.float32
    ) + jnp.einsum("mcd,cmk->dmk", weights[0], inputs[:, 1], preferred_element_type=jnp.float32)
    return jnp.stack([out_real, out_imag], axis=1)


def plain_body(state_field, spectral_weight, mode_gain, bypass_weight):
    fwd_lon, inv_lon, fwd_lat, inv_lat = make_tables()
    chan_count = state_field.shape[0]
    band_rows = state_field.shape[1]
    flat_field = state_field.reshape(chan_count * band_rows, LON)
    lon_spectrum = (
        jnp.dot(flat_field, fwd_lon.reshape(LON, 2 * M), preferred_element_type=jnp.float32)
        .astype(jnp.bfloat16)
        .reshape(chan_count, band_rows, 2, M)
    )
    all_latitudes = lax.all_to_all(lon_spectrum, "sp", split_axis=3, concat_axis=1, tiled=True)
    lat_parts = jnp.einsum(
        "clrm,lsk->crmsk", all_latitudes, fwd_lat, preferred_element_type=jnp.float32
    )
    real_part = lat_parts[:, 0, :, 0] + lat_parts[:, 1, :, 1]
    imag_part = lat_parts[:, 1, :, 0] - lat_parts[:, 0, :, 1]
    modes_in = jnp.stack([real_part, imag_part], axis=1).astype(jnp.bfloat16)
    weight_rows = lax.all_to_all(spectral_weight, "ch", split_axis=3, concat_axis=2, tiled=True)
    all_inputs = lax.all_gather(modes_in, "ch", axis=0, tiled=True)
    mixed = mix_modes(weight_rows, all_inputs)
    scaled = (mixed * mode_gain[:, None, None, :]).astype(jnp.bfloat16)
    back_parts = jnp.einsum("drmk,ksl->drmsl", scaled, inv_lat, preferred_element_type=jnp.float32)
    back_real = back_parts[:, 0, :, 0] - back_parts[:, 1, :, 1]
    back_imag = back_parts[:, 0, :, 1] + back_parts[:, 1, :, 0]
    lat_field = (jnp.stack([back_real, back_imag], axis=1) * (1.0 / LAT)).astype(jnp.bfloat16)
    band_spectrum = lax.all_to_all(lat_field, "sp", split_axis=3, concat_axis=2, tiled=True)
    spectral_out = jnp.einsum(
        "drml,rmx->dlx", band_spectrum, inv_lon, preferred_element_type=jnp.float32
    ) * (1.0 / LON)
    out_width = bypass_weight.shape[1] // lax.axis_size("ch")
    own_columns = lax.dynamic_slice_in_dim(
        bypass_weight, lax.axis_index("ch") * out_width, out_width, 1
    )
    bypass = jnp.einsum(
        "cd,clx->dlx",
        own_columns,
        lax.all_gather(state_field, "ch", axis=0, tiled=True),
        preferred_element_type=jnp.float32,
    ).astype(jnp.bfloat16)
    return jax.nn.gelu(spectral_out + bypass.astype(jnp.float32), approximate=False).astype(
        jnp.bfloat16
    )


def lon_table(n_sp, modes, transposed):
    col = np.arange(n_sp * 2 * modes)
    imag, mode = (col // modes) % 2, col // (2 * modes) * modes + col % modes
    angle = (np.arange(LON)[:, None] * mode[None, :]) % LON * (2.0 * math.pi / LON)
    value = np.where(imag == 0, np.cos(angle), -np.sin(angle))
    if transposed:
        value = (value * np.where(mode == 0, 1.0, 2.0)).T
    return jnp.asarray(value.astype(ml_dtypes.bfloat16))


def lat_table():
    k = np.arange(L)
    kappa = np.where(k < L // 2, k, k - L)
    angle = (np.arange(LAT)[:, None] * kappa[None, :]) % LAT * (2.0 * math.pi / LAT)
    value = np.zeros((LAT, 2, KPAD))
    value[:, 0, :L], value[:, 1, :L] = np.cos(angle), np.sin(angle)
    return jnp.asarray(value.reshape(LAT, 2 * KPAD).astype(ml_dtypes.bfloat16))


MAP_COST = [0, 0, 120, 0, 0]
CARRIED_COST = [120, 120, 40, 40]
CARRY = 20
LAT_COST = 150
OWN_COST = 50


def call(kernel, name, cost=0, **kwargs):
    return pl.pallas_call(
        kernel,
        name=name,
        compiler_params=pltpu.CompilerParams(vmem_limit_bytes=VMEM),
        cost_estimate=pl.CostEstimate(
            flops=1 + int(cost * 1e9), bytes_accessed=1, transcendentals=0
        ),
        **kwargs,
    )


def const_spec(shape):
    return pl.BlockSpec(shape, lambda *_: (0,) * len(shape))


def kron_map(weight):
    c, d = weight.shape
    high, wide = d * ROWS, c * ROWS

    def kernel(w_ref, out):
        iota = functools.partial(lax.broadcasted_iota, jnp.int32)
        left = (iota((high, d), 0) // ROWS == iota((high, d), 1)).astype(F32).astype(BF16)
        right = (iota((c, wide), 1) // ROWS == iota((c, wide), 0)).astype(F32).astype(BF16)
        tall = lax.dot_general(
            left, w_ref[...], (((1,), (1,)), ((), ())), preferred_element_type=F32
        ).astype(BF16)
        value = jnp.dot(tall, right, preferred_element_type=F32)
        same = iota((high, wide), 0) % ROWS == iota((high, wide), 1) % ROWS
        out[...] = jnp.where(same, value, 0.0).astype(BF16)

    return call(
        kernel, "kron_map", out_shape=jax.ShapeDtypeStruct((high, wide), BF16)
    )(weight)


def pick_weights(ch, own, sibling):
    _, modes, chans, _ = own.shape
    half = LANES // 2
    step = modes // 4

    def kernel(ch_ref, a0, a1, b0, b1, out):
        for parity in range(2):

            @pl.when(ch_ref[0] % 2 == parity)
            def _():
                cols = slice(parity * half, (parity + 1) * half)
                for i, pair in enumerate(((a0, a1), (b0, b1))):
                    out[:, :, i * chans : (i + 1) * chans, :] = jnp.concatenate(
                        [ref[:, :, :, cols] for ref in pair], axis=-1
                    )

    def tile(far):
        return pl.BlockSpec(
            (2, step, chans, LANES), lambda i, ch_ref: (0, i, 0, (ch_ref[0] // 2 + far) % 2)
        )

    return call(
        kernel,
        "pick_weights",
        grid_spec=pltpu.PrefetchScalarGridSpec(
            num_scalar_prefetch=1,
            grid=(modes // step,),
            in_specs=[tile(0), tile(1), tile(0), tile(1)],
            out_specs=pl.BlockSpec((2, step, 2 * chans, LANES), lambda i, ch_ref: (0, i, 0, 0)),
        ),
        out_shape=jax.ShapeDtypeStruct((2, modes, 2 * chans, LANES), BF16),
    )(ch.reshape(1), own, own, sibling, sibling)


def lon_forward(field, table, start, count, n_sp):
    rows = field.shape[1]
    step = 4

    def kernel(s_ref, t_ref, out):
        s = s_ref[...].reshape(step * rows, LON)
        acc = jnp.dot(s, t_ref[...], preferred_element_type=F32)
        for k in range(n_sp):
            part = acc[:, k * LANES : (k + 1) * LANES].astype(BF16)
            out[k] = part.reshape(step, rows, LANES)

    return call(
        kernel,
        "lon_forward",
        grid=(count // step,),
        in_specs=[
            pl.BlockSpec((step, rows, LON), lambda i: (start // step + i, 0, 0)),
            const_spec(table.shape),
        ],
        out_specs=pl.BlockSpec((n_sp, step, rows, LANES), lambda i: (0, i, 0, 0)),
        out_shape=jax.ShapeDtypeStruct((n_sp, count, rows, LANES), BF16),
    )(field, table)


def lat_forward(bands, table):
    n_sp, count, rows, _ = bands.shape
    step = ROWS
    half = LANES // 2

    def kernel(x_ref, t_ref, out, left, right):
        for c in range(step):
            x = x_ref[:, c].reshape(n_sp * rows, LANES)
            left[c * LANES : (c + 1) * LANES, :] = x.T
        for c in range(step):
            g = jnp.dot(
                left[c * LANES : (c + 1) * LANES, :], t_ref[...], preferred_element_type=F32
            )
            right[c, :half, :] = g[:half, :KPAD] + g[half:, KPAD:]
            right[c, half:, :] = g[half:, :KPAD] - g[:half, KPAD:]
        out[...] = jnp.transpose(right[...], (1, 0, 2)).astype(BF16)

    return call(
        kernel,
        "lat_forward",
        grid=(count // step,),
        in_specs=[
            pl.BlockSpec((n_sp, step, rows, LANES), lambda i: (0, i, 0, 0)),
            const_spec(table.shape),
        ],
        out_specs=pl.BlockSpec((LANES, step, KPAD), lambda i: (0, i, 0)),
        out_shape=jax.ShapeDtypeStruct((LANES, count, KPAD), BF16),
        scratch_shapes=[
            pltpu.VMEM((step * LANES, n_sp * rows), BF16),
            pltpu.VMEM((step, LANES, KPAD), F32),
        ],
    )(bands, table)


def mix(weights, spectra, parts):
    modes, chans, outs2 = weights.shape[1:]
    outs = outs2 // 2
    step = ROWS
    n_in = len(spectra)
    carry = outs - sum(parts)

    def kernel(w_ref, *refs):
        ins, own, carried, sends = refs[:n_in], refs[n_in], refs[n_in + 1], refs[n_in + 2 : -1]
        scratch = refs[-1]
        for m in range(step):
            y = jnp.concatenate([ref[r, m] for r in range(2) for ref in ins], axis=0)
            wr, wi = w_ref[0, m], w_ref[1, m]
            w = jnp.concatenate(
                [jnp.concatenate([wr, wi], axis=1), jnp.concatenate([-wi, wr], axis=1)], axis=0
            )
            scratch[m] = lax.dot_general(
                w, y, (((0,), (0,)), ((), ())), preferred_element_type=F32
            )
        for r in range(2):
            base = r * outs2
            own[r] = jnp.transpose(scratch[:, base : base + outs, :], (1, 0, 2))
        far = [
            jnp.transpose(scratch[:, r * outs2 + outs : (r + 1) * outs2, :], (1, 0, 2))
            for r in range(2)
        ]
        for r in range(2):
            carried[r] = far[r][outs - carry :]
        for i, send in enumerate(sends):
            block = [f[sum(parts[:i]) : sum(parts[: i + 1])] for f in far]
            for r in range(2):
                for t in range(2):
                    send[2 * r + t] = block[r][:, :, t * LANES : (t + 1) * LANES].astype(BF16)
            tail = [b[:, :, 2 * LANES : 2 * LANES + LANES // 2] for b in block]
            send[4] = jnp.concatenate(tail, axis=-1).astype(BF16)

    res = call(
        kernel,
        "mix",
        grid=(modes // step,),
        in_specs=[pl.BlockSpec((2, step, chans, outs2), lambda i: (0, i, 0, 0))]
        + [pl.BlockSpec((2, step, s.shape[2], KPAD), lambda i: (0, i, 0, 0)) for s in spectra],
        out_specs=[pl.BlockSpec((2, n, step, KPAD), lambda i: (0, 0, i, 0)) for n in (outs, carry)]
        + [pl.BlockSpec((5, per, step, LANES), lambda i: (0, 0, i, 0)) for per in parts],
        out_shape=[jax.ShapeDtypeStruct((2, n, modes, KPAD), F32) for n in (outs, carry)]
        + [jax.ShapeDtypeStruct((5, per, modes, LANES), BF16) for per in parts],
        scratch_shapes=[pltpu.VMEM((step, 2 * outs2, KPAD), F32)],
    )(weights, *spectra)
    return res[0], res[1], res[2:]


def lat_backward(own, far, gain, table, start, per, n_sp, cost=0):
    modes = own.shape[2]
    rows = LAT // n_sp
    step = 4

    def kernel(own_ref, *refs):
        far_ref = refs[0] if far is not None else None
        g_ref, t_ref, result = refs[-3:]
        for pair in range(step // 2):
            blocks = []
            for d in (2 * pair, 2 * pair + 1):
                z = []
                for r in range(2):
                    if far_ref is None:
                        z.append((own_ref[r, d] * g_ref[d]).astype(BF16))
                        continue
                    tail = far_ref[4, d][:, r * (LANES // 2) : (r + 1) * (LANES // 2)]
                    sent = jnp.concatenate(
                        [
                            far_ref[2 * r, d].astype(F32),
                            far_ref[2 * r + 1, d].astype(F32),
                            tail.astype(F32),
                            jnp.zeros((modes, LANES // 2), F32),
                        ],
                        axis=-1,
                    )
                    z.append(((own_ref[r, d] + sent) * g_ref[d]).astype(BF16))
                blocks.append(jnp.concatenate([z[0], -z[1]], axis=1))
                blocks.append(jnp.concatenate([z[1], z[0]], axis=1))
            both = jnp.concatenate(blocks, axis=0)
            out = lax.dot_general(
                t_ref[...], both, (((1,), (1,)), ((), ())), preferred_element_type=F32
            ) * (1.0 / LAT)
            for k in range(n_sp):
                for i in range(2):
                    result[k, 2 * pair + i] = out[
                        k * rows : (k + 1) * rows, i * LANES : (i + 1) * LANES
                    ].astype(BF16)

    return call(
        kernel,
        "lat_backward",
        cost,
        grid=(per // step,),
        in_specs=[
            pl.BlockSpec((2, step, modes, KPAD), lambda i: (0, start // step + i, 0, 0)),
        ]
        + [pl.BlockSpec((5, step, modes, LANES), lambda i: (0, i, 0, 0))] * (far is not None)
        + [
            pl.BlockSpec((step, 1, KPAD), lambda i: (start // step + i, 0, 0)),
            const_spec(table.shape),
        ],
        out_specs=pl.BlockSpec((n_sp, step, rows, LANES), lambda i: (0, i, 0, 0)),
        out_shape=jax.ShapeDtypeStruct((n_sp, per, rows, LANES), BF16),
    )(*([own] if far is None else [own, far]), gain, table)


WIDE = 2 * LANES
FULL = LON // WIDE
REST = LON - FULL * WIDE
TAIL = REST - LANES


def partial_map(field, sibling, kron, start, steps, cost, spectrum=None, table=None):
    chans = field.shape[0]
    outs = kron.shape[0] // ROWS
    height = outs * ROWS
    depth = chans * ROWS
    packed = height * LON // LANES
    group = LANES // TAIL

    n_sp = spectrum.shape[0] if spectrum is not None else 0

    def kernel(a_ref, b_ref, w_ref, *refs):
        out = refs[2] if n_sp else refs[0]
        if n_sp:
            s_ref, t_ref, _, lat = refs
            for k in range(n_sp):
                lat[:, k * LANES : (k + 1) * LANES] = s_ref[k].reshape(height, LANES)

        def product(cols, width):
            a = a_ref[:, :, cols].reshape(depth, width)
            b = b_ref[:, :, cols].reshape(depth, width)
            acc = jnp.dot(w_ref[:, :depth], a, preferred_element_type=F32) + jnp.dot(
                w_ref[:, depth:], b, preferred_element_type=F32
            )
            if n_sp:
                spectral = jnp.dot(lat[...], t_ref[:, cols], preferred_element_type=F32)
                acc = acc + spectral * (1.0 / LON)
            return acc

        @pl.loop(0, FULL)
        def _(n):
            acc = product(pl.ds(pl.multiple_of(n * WIDE, WIDE), WIDE), WIDE).astype(BF16)
            base = pl.multiple_of(n * 2 * height, 2 * height)
            out[0, pl.ds(base, height), :] = acc[:, :LANES]
            out[0, pl.ds(base + height, height), :] = acc[:, LANES:]

        acc = product(slice(FULL * WIDE, LON), REST)
        out[0, FULL * 2 * height : (FULL * 2 + 1) * height, :] = acc[:, :LANES].astype(BF16)
        tail = acc[:, LANES:]
        size = height // group
        out[0, (FULL * 2 + 1) * height :, :] = jnp.concatenate(
            [tail[q * size : (q + 1) * size] for q in range(group)], axis=1
        ).astype(BF16)

    sib_start = start if sibling.shape[1] == field.shape[1] else 0
    return call(
        kernel,
        "partial_map",
        cost,
        grid=(steps,),
        in_specs=[
            pl.BlockSpec((chans, ROWS, LON), lambda i: (0, start + i, 0)),
            pl.BlockSpec((chans, ROWS, LON), lambda i: (0, sib_start + i, 0)),
            const_spec(kron.shape),
        ]
        + (
            [
                pl.BlockSpec((n_sp, outs, ROWS, LANES), lambda i: (0, 0, start + i, 0)),
                const_spec(table.shape),
            ]
            if n_sp
            else []
        ),
        out_specs=pl.BlockSpec((1, packed, LANES), lambda i: (i, 0, 0)),
        out_shape=jax.ShapeDtypeStruct((steps, packed, LANES), BF16),
        scratch_shapes=[pltpu.VMEM((height, n_sp * LANES), BF16)] if n_sp else [],
    )(field, sibling, kron, *([spectrum, table] if n_sp else []))


def own_map(field, sibling, kron, start, steps, cost=0):
    chans = field.shape[0]
    outs = kron.shape[0] // ROWS
    depth = chans * ROWS

    def kernel(a_ref, b_ref, w_ref, out):
        def product(cols, width):
            a = a_ref[:, :, cols].reshape(depth, width)
            b = b_ref[:, :, cols].reshape(depth, width)
            acc = jnp.dot(w_ref[:, :depth], a, preferred_element_type=F32) + jnp.dot(
                w_ref[:, depth:], b, preferred_element_type=F32
            )
            out[:, :, cols] = acc.reshape(outs, ROWS, width)

        @pl.loop(0, FULL)
        def _(n):
            product(pl.ds(pl.multiple_of(n * WIDE, WIDE), WIDE), WIDE)

        product(slice(FULL * WIDE, LON), REST)

    rows = pl.BlockSpec((chans, ROWS, LON), lambda i: (0, start + i, 0))
    return call(
        kernel,
        "own_map",
        cost,
        grid=(steps,),
        in_specs=[rows, rows, const_spec(kron.shape)],
        out_specs=pl.BlockSpec((outs, ROWS, LON), lambda i: (0, i, 0)),
        out_shape=jax.ShapeDtypeStruct((outs, steps * ROWS, LON), F32),
    )(field, sibling, kron)


def gelu(v):
    return 0.5 * v * (1.0 + lax.erf(v * math.sqrt(0.5)))


def finish(previous, own, spectrum, table, received, start, steps, own_start, shape):
    outs = own.shape[0]
    height = outs * ROWS
    group = LANES // TAIL
    heights = [got.shape[1] * LANES // LON for got, _ in received]
    n_sp = spectrum[0].shape[0]
    sizes = [part.shape[1] for part in spectrum]

    def kernel(*refs):
        refs = refs[1:] if previous is not None else refs
        o_ref, t_ref = refs[:2]
        packs, lats = refs[2 : 2 + len(received)], refs[2 + len(received) : -2]
        out, lat = refs[-2], refs[-1]
        at = 0
        for ref, per in zip(lats, sizes):
            for k in range(n_sp):
                lat[at : at + per * ROWS, k * LANES : (k + 1) * LANES] = ref[k].reshape(
                    per * ROWS, LANES
                )
            at += per * ROWS

        def product(cols, width):
            spectral = jnp.dot(lat[...], t_ref[:, cols], preferred_element_type=F32)
            return spectral * (1.0 / LON) + o_ref[:, :, cols].reshape(height, width)

        @pl.loop(0, FULL)
        def _(n):
            cols = pl.ds(pl.multiple_of(n * WIDE, WIDE), WIDE)
            acc = product(cols, WIDE)
            far = []
            for p_ref, high in zip(packs, heights):
                base = pl.multiple_of(n * 2 * high, 2 * high)
                far.append([p_ref[0, pl.ds(base + i * high, high), :] for i in range(2)])
            far = jnp.concatenate([jnp.concatenate(pair, axis=1) for pair in far], axis=0)
            value = gelu(acc + far.astype(F32)).astype(BF16)
            out[:, :, cols] = value.reshape(outs, ROWS, WIDE)

        acc = product(slice(FULL * WIDE, LON), REST)
        far, tail = [], []
        for p_ref, high in zip(packs, heights):
            far.append(p_ref[0, FULL * 2 * high : (FULL * 2 + 1) * high, :])
            tails = p_ref[0, (FULL * 2 + 1) * high :, :].astype(F32)
            tail += [tails[:, q * TAIL : (q + 1) * TAIL] for q in range(group)]
        far = jnp.concatenate(far, axis=0).astype(F32)
        tail = jnp.concatenate(tail, axis=0)
        one = gelu(acc[:, :LANES] + far).astype(BF16)
        out[:, :, FULL * WIDE : FULL * WIDE + LANES] = one.reshape(outs, ROWS, LANES)
        two = gelu(acc[:, LANES:] + tail).astype(BF16)
        out[:, :, FULL * WIDE + LANES :] = two.reshape(outs, ROWS, TAIL)

    operands = [own, table, *[got for got, _ in received], *spectrum]
    specs = [
        pl.BlockSpec((outs, ROWS, LON), lambda i: (0, own_start + i, 0)),
        const_spec(table.shape),
    ] + [
        pl.BlockSpec((1, got.shape[1], LANES), functools.partial(lambda first, i: (first + i, 0, 0), first))
        for got, first in received
    ] + [
        pl.BlockSpec((n_sp, per, ROWS, LANES), lambda i: (0, 0, start + i, 0)) for per in sizes
    ]
    aliases = {}
    if previous is not None:
        operands = [previous] + operands
        specs = [pl.BlockSpec(memory_space=pl.ANY)] + specs
        aliases = {0: 0}
    return call(
        kernel,
        "finish",
        grid=(steps,),
        in_specs=specs,
        out_specs=pl.BlockSpec((outs, ROWS, LON), lambda i: (0, start + i, 0)),
        out_shape=jax.ShapeDtypeStruct(shape, BF16),
        input_output_aliases=aliases,
        scratch_shapes=[pltpu.VMEM((height, n_sp * LANES), BF16)],
    )(*operands)


def after(value, *others):
    return lax.optimization_barrier((value, *others))[0]


def row_plan(total):
    unit = total // 12
    last = total - 11 * unit
    return [2 * unit, 3 * unit, 3 * unit, 3 * unit, last], [4 * unit, 4 * unit, 3 * unit, last]


def tiled_body(state_field, spectral_weight, mode_gain, bypass_weight):
    chans, rows, _ = state_field.shape
    modes = spectral_weight.shape[1]
    n_sp, n_ch = lax.axis_size("sp"), lax.axis_size("ch")
    ch = lax.axis_index("ch")
    near, far = jnp.bitwise_xor(ch, 1), jnp.bitwise_xor(ch, 2)

    def to_near(value):
        return lax.ppermute(value, "ch", [(i, i ^ 1) for i in range(n_ch)])

    def to_far(value):
        return lax.ppermute(value, "ch", [(i, i ^ 2) for i in range(n_ch)])

    def across(blocks):
        return lax.all_to_all(blocks, "sp", 0, 0)

    plan, carried_plan = row_plan(rows // ROWS)
    plain = chans - CARRY

    near_first = to_near(lax.slice_in_dim(state_field, 0, plan[0] * ROWS, axis=1))

    def rows_of(index):
        return lax.dynamic_slice_in_dim(bypass_weight, index * chans, chans, 0)

    chip_rows = jnp.concatenate([rows_of(ch), rows_of(near)], axis=0)
    far_columns = lax.dynamic_slice_in_dim(chip_rows, far * chans, chans, 1)
    kron_far = kron_map(far_columns[:, :plain])
    near_field = to_near(after(state_field, near_first, kron_far))
    near_weight = to_near(after(spectral_weight, near_first))

    sent, received = [], []

    def partial_rows(*others):
        i = len(sent)
        sibling = near_field if i else near_first
        kron = after(kron_far, *others)
        sent.append(partial_map(state_field, sibling, kron, sum(plan[:i]), plan[i], MAP_COST[i]))

    def send_rows(*others):
        received.append(to_far(after(sent[len(received)], *others)))

    half = chans // 2
    table = lon_table(n_sp, modes, False)
    inverse = lon_table(n_sp, modes, True)
    lat = lat_table()
    gain = jnp.pad(mode_gain, ((0, 0), (0, KPAD - L))).reshape(chans, 1, KPAD)
    far_gain = to_far(gain)
    partial_rows()
    send_rows(far_gain)
    bands = [lon_forward(state_field, after(table, sent[0]), 0, half, n_sp)]
    partial_rows(bands[0])
    send_rows(received[0])
    partial_rows(sent[1])
    send_rows(received[1])
    bands.append(lon_forward(state_field, after(table, sent[2]), half, half, n_sp))
    kron_own = kron_map(lax.dynamic_slice_in_dim(chip_rows, ch * chans, chans, 1))
    kron_carried = kron_map(far_columns[:, plain:])
    middle = plan[0]
    own = [own_map(state_field, near_field, after(kron_own, sent[2]), 0, middle)]
    bands[1] = after(bands[1], sent[2], own[0])
    weights = pick_weights(ch, spectral_weight, near_weight)
    carried_gain = after(far_gain, weights)[plain:]
    bands = [across(b) for b in bands]
    spectra = [lat_forward(bands[0], lat)]
    own.append(own_map(state_field, near_field, after(kron_own, spectra[0]), middle, sum(plan[1:]), OWN_COST))
    spectra.append(lat_forward(bands[1], after(lat, own[1], weights, kron_carried, carried_gain)))
    spectra = [s.reshape(2, modes, -1, KPAD) for s in spectra]
    near_spectra = [to_near(s) for s in spectra]

    parts = [plain - 16, 16]
    own_mixed, carried, sends = mix(weights, spectra + near_spectra, parts)
    far_mixed = [to_far(after(s, received[2])) for s in sends]
    carried = lat_backward(carried, None, carried_gain, lat, 0, CARRY, n_sp)
    carried = across(carried)

    back = [
        lat_backward(own_mixed, None, gain, lat, plain, CARRY, n_sp),
        lat_backward(own_mixed, far_mixed[0], gain, lat, 0, parts[0], n_sp),
        lat_backward(own_mixed, far_mixed[1], gain, lat, parts[0], parts[1], n_sp, LAT_COST),
    ]
    spectrum = []
    for b in back:
        spectrum.append(across(after(b, spectrum[-1] if spectrum else carried)))
    spectrum = spectrum[1:] + spectrum[:1]
    for _ in range(2):
        partial_rows(*sends)
        send_rows(far_mixed[1])

    kron_carried = after(kron_carried, back[2])
    late = []
    for i, steps in enumerate(carried_plan):
        at = sum(carried_plan[:i])
        block = partial_map(
            state_field, near_field, kron_carried, at, steps, CARRIED_COST[i], carried, inverse
        )
        late.append(to_far(after(block, late[0] if i > 1 else received[4 - i])))

    out = None
    cuts = sorted({sum(p[:i]) for p in (plan, carried_plan) for i in range(len(p) + 1)})
    for start, end in zip(cuts, cuts[1:]):
        got = []
        for blocks, p in ((received, plan), (late, carried_plan)):
            i = max(i for i in range(len(p)) if sum(p[:i]) <= start)
            got.append((blocks[i], start - sum(p[:i])))
        part = start >= middle
        out = finish(
            out, own[part], spectrum, inverse, got, start, end - start, start - part * middle,
            state_field.shape,
        )
    return out


def body(state_field, spectral_weight, mode_gain, bypass_weight):
    chans, rows, _ = state_field.shape
    modes = spectral_weight.shape[1]
    n_sp, n_ch = lax.axis_size("sp"), lax.axis_size("ch")
    whole_tiles = (
        n_ch == 4
        and 2 * modes == LANES
        and chans == 64
        and rows % (12 * ROWS) == 0
    )
    run = tiled_body if whole_tiles else plain_body
    return run(state_field, spectral_weight, mode_gain, bypass_weight)


def solution(mesh):
    in_specs = (P(("grp", "ch"), "sp", None), P(None, "sp", "ch", None), P("ch", None), P())
    out_specs = P(("grp", "ch"), "sp", None)
    return jax.shard_map(body, mesh=mesh, in_specs=in_specs, out_specs=out_specs, check_vma=False)
```

```python
import functools
import math

import jax
import jax.numpy as jnp
import ml_dtypes
import numpy as np
from jax import lax
from jax.experimental import pallas as pl
from jax.experimental.pallas import tpu as pltpu
from jax.sharding import PartitionSpec as P

LAT = 768
LON = 1440
M = 256
L = 320

LANES = 128
ROWS = 16
KPAD = 384
VMEM = 56 * 1024 * 1024
F32 = jnp.float32
BF16 = jnp.bfloat16


def make_tables():
    lon_index = jnp.arange(LON, dtype=jnp.int32)
    mode_index = jnp.arange(M, dtype=jnp.int32)
    phase_lon = jnp.mod(lon_index[:, None] * mode_index[None, :], LON).astype(jnp.float32) * (
        2.0 * math.pi / LON
    )
    fwd_lon = jnp.stack([jnp.cos(phase_lon), -jnp.sin(phase_lon)], axis=1).astype(jnp.bfloat16)
    mode_weight = jnp.where(mode_index == 0, 1.0, 2.0).astype(jnp.float32)
    inv_lon = jnp.stack(
        [mode_weight[:, None] * jnp.cos(phase_lon).T, -mode_weight[:, None] * jnp.sin(phase_lon).T],
        axis=0,
    ).astype(jnp.bfloat16)
    lat_index = jnp.arange(LAT, dtype=jnp.int32)
    wave_index = jnp.arange(L, dtype=jnp.int32)
    wave_number = jnp.where(wave_index < L // 2, wave_index, wave_index - L)
    phase_lat = jnp.mod(lat_index[:, None] * wave_number[None, :], LAT).astype(jnp.float32) * (
        2.0 * math.pi / LAT
    )
    fwd_lat = jnp.stack([jnp.cos(phase_lat), jnp.sin(phase_lat)], axis=1).astype(jnp.bfloat16)
    inv_lat = jnp.stack([jnp.cos(phase_lat).T, jnp.sin(phase_lat).T], axis=1).astype(jnp.bfloat16)
    return (fwd_lon, inv_lon, fwd_lat, inv_lat)


def mix_modes(weights, inputs):
    out_real = jnp.einsum(
        "mcd,cmk->dmk", weights[0], inputs[:, 0], preferred_element_type=jnp.float32
    ) - jnp.einsum("mcd,cmk->dmk", weights[1], inputs[:, 1], preferred_element_type=jnp.float32)
    out_imag = jnp.einsum(
        "mcd,cmk->dmk", weights[1], inputs[:, 0], preferred_element_type=jnp.float32
    ) + jnp.einsum("mcd,cmk->dmk", weights[0], inputs[:, 1], preferred_element_type=jnp.float32)
    return jnp.stack([out_real, out_imag], axis=1)


def plain_body(state_field, spectral_weight, mode_gain, bypass_weight):
    fwd_lon, inv_lon, fwd_lat, inv_lat = make_tables()
    chan_count = state_field.shape[0]
    band_rows = state_field.shape[1]
    flat_field = state_field.reshape(chan_count * band_rows, LON)
    lon_spectrum = (
        jnp.dot(flat_field, fwd_lon.reshape(LON, 2 * M), preferred_element_type=jnp.float32)
        .astype(jnp.bfloat16)
        .reshape(chan_count, band_rows, 2, M)
    )
    all_latitudes = lax.all_to_all(lon_spectrum, "sp", split_axis=3, concat_axis=1, tiled=True)
    lat_parts = jnp.einsum(
        "clrm,lsk->crmsk", all_latitudes, fwd_lat, preferred_element_type=jnp.float32
    )
    real_part = lat_parts[:, 0, :, 0] + lat_parts[:, 1, :, 1]
    imag_part = lat_parts[:, 1, :, 0] - lat_parts[:, 0, :, 1]
    modes_in = jnp.stack([real_part, imag_part], axis=1).astype(jnp.bfloat16)
    weight_rows = lax.all_to_all(spectral_weight, "ch", split_axis=3, concat_axis=2, tiled=True)
    all_inputs = lax.all_gather(modes_in, "ch", axis=0, tiled=True)
    mixed = mix_modes(weight_rows, all_inputs)
    scaled = (mixed * mode_gain[:, None, None, :]).astype(jnp.bfloat16)
    back_parts = jnp.einsum("drmk,ksl->drmsl", scaled, inv_lat, preferred_element_type=jnp.float32)
    back_real = back_parts[:, 0, :, 0] - back_parts[:, 1, :, 1]
    back_imag = back_parts[:, 0, :, 1] + back_parts[:, 1, :, 0]
    lat_field = (jnp.stack([back_real, back_imag], axis=1) * (1.0 / LAT)).astype(jnp.bfloat16)
    band_spectrum = lax.all_to_all(lat_field, "sp", split_axis=3, concat_axis=2, tiled=True)
    spectral_out = jnp.einsum(
        "drml,rmx->dlx", band_spectrum, inv_lon, preferred_element_type=jnp.float32
    ) * (1.0 / LON)
    out_width = bypass_weight.shape[1] // lax.axis_size("ch")
    own_columns = lax.dynamic_slice_in_dim(
        bypass_weight, lax.axis_index("ch") * out_width, out_width, 1
    )
    bypass = jnp.einsum(
        "cd,clx->dlx",
        own_columns,
        lax.all_gather(state_field, "ch", axis=0, tiled=True),
        preferred_element_type=jnp.float32,
    ).astype(jnp.bfloat16)
    return jax.nn.gelu(spectral_out + bypass.astype(jnp.float32), approximate=False).astype(
        jnp.bfloat16
    )


def lon_table(n_sp, modes, transposed):
    col = np.arange(n_sp * 2 * modes)
    imag, mode = (col // modes) % 2, col // (2 * modes) * modes + col % modes
    angle = (np.arange(LON)[:, None] * mode[None, :]) % LON * (2.0 * math.pi / LON)
    value = np.where(imag == 0, np.cos(angle), -np.sin(angle))
    if transposed:
        value = (value * np.where(mode == 0, 1.0, 2.0)).T
    return jnp.asarray(value.astype(ml_dtypes.bfloat16))


def lat_table():
    k = np.arange(L)
    kappa = np.where(k < L // 2, k, k - L)
    angle = (np.arange(LAT)[:, None] * kappa[None, :]) % LAT * (2.0 * math.pi / LAT)
    value = np.zeros((LAT, 2, KPAD))
    value[:, 0, :L], value[:, 1, :L] = np.cos(angle), np.sin(angle)
    return jnp.asarray(value.reshape(LAT, 2 * KPAD).astype(ml_dtypes.bfloat16))


MAP_COST = [0, 0, 0, 120, 0, 0]
CARRIED_COST = [120, 120, 40, 40]
CARRY = 20
LAT_COST = 150
OWN_COST = 50


def call(kernel, name, cost=0, **kwargs):
    return pl.pallas_call(
        kernel,
        name=name,
        compiler_params=pltpu.CompilerParams(vmem_limit_bytes=VMEM),
        cost_estimate=pl.CostEstimate(
            flops=1 + int(cost * 1e9), bytes_accessed=1, transcendentals=0
        ),
        **kwargs,
    )


def const_spec(shape):
    return pl.BlockSpec(shape, lambda *_: (0,) * len(shape))


def kron_map(weight):
    c, d = weight.shape
    high, wide = d * ROWS, c * ROWS

    def kernel(w_ref, out):
        iota = functools.partial(lax.broadcasted_iota, jnp.int32)
        left = (iota((high, d), 0) // ROWS == iota((high, d), 1)).astype(F32).astype(BF16)
        right = (iota((c, wide), 1) // ROWS == iota((c, wide), 0)).astype(F32).astype(BF16)
        tall = lax.dot_general(
            left, w_ref[...], (((1,), (1,)), ((), ())), preferred_element_type=F32
        ).astype(BF16)
        value = jnp.dot(tall, right, preferred_element_type=F32)
        same = iota((high, wide), 0) % ROWS == iota((high, wide), 1) % ROWS
        out[...] = jnp.where(same, value, 0.0).astype(BF16)

    return call(
        kernel, "kron_map", out_shape=jax.ShapeDtypeStruct((high, wide), BF16)
    )(weight)


def pick_weights(ch, own, sibling):
    _, modes, chans, _ = own.shape
    half = LANES // 2
    step = modes // 4

    def kernel(ch_ref, a0, a1, b0, b1, out):
        for parity in range(2):

            @pl.when(ch_ref[0] % 2 == parity)
            def _():
                cols = slice(parity * half, (parity + 1) * half)
                for i, pair in enumerate(((a0, a1), (b0, b1))):
                    out[:, :, i * chans : (i + 1) * chans, :] = jnp.concatenate(
                        [ref[:, :, :, cols] for ref in pair], axis=-1
                    )

    def tile(far):
        return pl.BlockSpec(
            (2, step, chans, LANES), lambda i, ch_ref: (0, i, 0, (ch_ref[0] // 2 + far) % 2)
        )

    return call(
        kernel,
        "pick_weights",
        grid_spec=pltpu.PrefetchScalarGridSpec(
            num_scalar_prefetch=1,
            grid=(modes // step,),
            in_specs=[tile(0), tile(1), tile(0), tile(1)],
            out_specs=pl.BlockSpec((2, step, 2 * chans, LANES), lambda i, ch_ref: (0, i, 0, 0)),
        ),
        out_shape=jax.ShapeDtypeStruct((2, modes, 2 * chans, LANES), BF16),
    )(ch.reshape(1), own, own, sibling, sibling)


def lon_forward(field, table, start, count, n_sp):
    rows = field.shape[1]
    step = 4

    def kernel(s_ref, t_ref, out):
        s = s_ref[...].reshape(step * rows, LON)
        acc = jnp.dot(s, t_ref[...], preferred_element_type=F32)
        for k in range(n_sp):
            part = acc[:, k * LANES : (k + 1) * LANES].astype(BF16)
            out[k] = part.reshape(step, rows, LANES)

    return call(
        kernel,
        "lon_forward",
        grid=(count // step,),
        in_specs=[
            pl.BlockSpec((step, rows, LON), lambda i: (start // step + i, 0, 0)),
            const_spec(table.shape),
        ],
        out_specs=pl.BlockSpec((n_sp, step, rows, LANES), lambda i: (0, i, 0, 0)),
        out_shape=jax.ShapeDtypeStruct((n_sp, count, rows, LANES), BF16),
    )(field, table)


def lat_forward(bands, table):
    n_sp, count, rows, _ = bands.shape
    step = ROWS
    half = LANES // 2

    def kernel(x_ref, t_ref, out, left, right):
        for c in range(step):
            x = x_ref[:, c].reshape(n_sp * rows, LANES)
            left[c * LANES : (c + 1) * LANES, :] = x.T
        for c in range(step):
            g = jnp.dot(
                left[c * LANES : (c + 1) * LANES, :], t_ref[...], preferred_element_type=F32
            )
            right[c, :half, :] = g[:half, :KPAD] + g[half:, KPAD:]
            right[c, half:, :] = g[half:, :KPAD] - g[:half, KPAD:]
        out[...] = jnp.transpose(right[...], (1, 0, 2)).astype(BF16)

    return call(
        kernel,
        "lat_forward",
        grid=(count // step,),
        in_specs=[
            pl.BlockSpec((n_sp, step, rows, LANES), lambda i: (0, i, 0, 0)),
            const_spec(table.shape),
        ],
        out_specs=pl.BlockSpec((LANES, step, KPAD), lambda i: (0, i, 0)),
        out_shape=jax.ShapeDtypeStruct((LANES, count, KPAD), BF16),
        scratch_shapes=[
            pltpu.VMEM((step * LANES, n_sp * rows), BF16),
            pltpu.VMEM((step, LANES, KPAD), F32),
        ],
    )(bands, table)


def mix(weights, spectra, parts):
    modes, chans, outs2 = weights.shape[1:]
    outs = outs2 // 2
    step = ROWS
    n_in = len(spectra)
    carry = outs - sum(parts)

    def kernel(w_ref, *refs):
        ins, own, carried, sends = refs[:n_in], refs[n_in], refs[n_in + 1], refs[n_in + 2 : -1]
        scratch = refs[-1]
        for m in range(step):
            y = jnp.concatenate([ref[r, m] for r in range(2) for ref in ins], axis=0)
            wr, wi = w_ref[0, m], w_ref[1, m]
            w = jnp.concatenate(
                [jnp.concatenate([wr, wi], axis=1), jnp.concatenate([-wi, wr], axis=1)], axis=0
            )
            scratch[m] = lax.dot_general(
                w, y, (((0,), (0,)), ((), ())), preferred_element_type=F32
            )
        for r in range(2):
            base = r * outs2
            own[r] = jnp.transpose(scratch[:, base : base + outs, :], (1, 0, 2))
        far = [
            jnp.transpose(scratch[:, r * outs2 + outs : (r + 1) * outs2, :], (1, 0, 2))
            for r in range(2)
        ]
        for r in range(2):
            carried[r] = far[r][outs - carry :]
        for i, send in enumerate(sends):
            block = [f[sum(parts[:i]) : sum(parts[: i + 1])] for f in far]
            for r in range(2):
                for t in range(2):
                    send[2 * r + t] = block[r][:, :, t * LANES : (t + 1) * LANES].astype(BF16)
            tail = [b[:, :, 2 * LANES : 2 * LANES + LANES // 2] for b in block]
            send[4] = jnp.concatenate(tail, axis=-1).astype(BF16)

    res = call(
        kernel,
        "mix",
        grid=(modes // step,),
        in_specs=[pl.BlockSpec((2, step, chans, outs2), lambda i: (0, i, 0, 0))]
        + [pl.BlockSpec((2, step, s.shape[2], KPAD), lambda i: (0, i, 0, 0)) for s in spectra],
        out_specs=[pl.BlockSpec((2, n, step, KPAD), lambda i: (0, 0, i, 0)) for n in (outs, carry)]
        + [pl.BlockSpec((5, per, step, LANES), lambda i: (0, 0, i, 0)) for per in parts],
        out_shape=[jax.ShapeDtypeStruct((2, n, modes, KPAD), F32) for n in (outs, carry)]
        + [jax.ShapeDtypeStruct((5, per, modes, LANES), BF16) for per in parts],
        scratch_shapes=[pltpu.VMEM((step, 2 * outs2, KPAD), F32)],
    )(weights, *spectra)
    return res[0], res[1], res[2:]


def lat_backward(own, far, gain, table, start, per, n_sp, cost=0):
    modes = own.shape[2]
    rows = LAT // n_sp
    step = 4

    def kernel(own_ref, *refs):
        far_ref = refs[0] if far is not None else None
        g_ref, t_ref, result = refs[-3:]
        for pair in range(step // 2):
            blocks = []
            for d in (2 * pair, 2 * pair + 1):
                z = []
                for r in range(2):
                    if far_ref is None:
                        z.append((own_ref[r, d] * g_ref[d]).astype(BF16))
                        continue
                    tail = far_ref[4, d][:, r * (LANES // 2) : (r + 1) * (LANES // 2)]
                    sent = jnp.concatenate(
                        [
                            far_ref[2 * r, d].astype(F32),
                            far_ref[2 * r + 1, d].astype(F32),
                            tail.astype(F32),
                            jnp.zeros((modes, LANES // 2), F32),
                        ],
                        axis=-1,
                    )
                    z.append(((own_ref[r, d] + sent) * g_ref[d]).astype(BF16))
                blocks.append(jnp.concatenate([z[0], -z[1]], axis=1))
                blocks.append(jnp.concatenate([z[1], z[0]], axis=1))
            both = jnp.concatenate(blocks, axis=0)
            out = lax.dot_general(
                t_ref[...], both, (((1,), (1,)), ((), ())), preferred_element_type=F32
            ) * (1.0 / LAT)
            for k in range(n_sp):
                for i in range(2):
                    result[k, 2 * pair + i] = out[
                        k * rows : (k + 1) * rows, i * LANES : (i + 1) * LANES
                    ].astype(BF16)

    return call(
        kernel,
        "lat_backward",
        cost,
        grid=(per // step,),
        in_specs=[
            pl.BlockSpec((2, step, modes, KPAD), lambda i: (0, start // step + i, 0, 0)),
        ]
        + [pl.BlockSpec((5, step, modes, LANES), lambda i: (0, i, 0, 0))] * (far is not None)
        + [
            pl.BlockSpec((step, 1, KPAD), lambda i: (start // step + i, 0, 0)),
            const_spec(table.shape),
        ],
        out_specs=pl.BlockSpec((n_sp, step, rows, LANES), lambda i: (0, i, 0, 0)),
        out_shape=jax.ShapeDtypeStruct((n_sp, per, rows, LANES), BF16),
    )(*([own] if far is None else [own, far]), gain, table)


WIDE = 2 * LANES
FULL = LON // WIDE
REST = LON - FULL * WIDE
TAIL = REST - LANES


def partial_map(field, sibling, kron, start, steps, cost, spectrum=None, table=None):
    chans = field.shape[0]
    outs = kron.shape[0] // ROWS
    height = outs * ROWS
    depth = chans * ROWS
    packed = height * LON // LANES
    group = LANES // TAIL

    n_sp = spectrum.shape[0] if spectrum is not None else 0

    def kernel(a_ref, b_ref, w_ref, *refs):
        out = refs[2] if n_sp else refs[0]
        if n_sp:
            s_ref, t_ref, _, lat = refs
            for k in range(n_sp):
                lat[:, k * LANES : (k + 1) * LANES] = s_ref[k].reshape(height, LANES)

        def product(cols, width):
            a = a_ref[:, :, cols].reshape(depth, width)
            b = b_ref[:, :, cols].reshape(depth, width)
            acc = jnp.dot(w_ref[:, :depth], a, preferred_element_type=F32) + jnp.dot(
                w_ref[:, depth:], b, preferred_element_type=F32
            )
            if n_sp:
                spectral = jnp.dot(lat[...], t_ref[:, cols], preferred_element_type=F32)
                acc = acc + spectral * (1.0 / LON)
            return acc

        @pl.loop(0, FULL)
        def _(n):
            acc = product(pl.ds(pl.multiple_of(n * WIDE, WIDE), WIDE), WIDE).astype(BF16)
            base = pl.multiple_of(n * 2 * height, 2 * height)
            out[0, pl.ds(base, height), :] = acc[:, :LANES]
            out[0, pl.ds(base + height, height), :] = acc[:, LANES:]

        acc = product(slice(FULL * WIDE, LON), REST)
        out[0, FULL * 2 * height : (FULL * 2 + 1) * height, :] = acc[:, :LANES].astype(BF16)
        tail = acc[:, LANES:]
        size = height // group
        out[0, (FULL * 2 + 1) * height :, :] = jnp.concatenate(
            [tail[q * size : (q + 1) * size] for q in range(group)], axis=1
        ).astype(BF16)

    return call(
        kernel,
        "partial_map",
        cost,
        grid=(steps,),
        in_specs=[
            pl.BlockSpec((chans, ROWS, LON), lambda i: (0, start + i, 0)),
            pl.BlockSpec((chans, ROWS, LON), lambda i: (0, start + i, 0)),
            const_spec(kron.shape),
        ]
        + (
            [
                pl.BlockSpec((n_sp, outs, ROWS, LANES), lambda i: (0, 0, start + i, 0)),
                const_spec(table.shape),
            ]
            if n_sp
            else []
        ),
        out_specs=pl.BlockSpec((1, packed, LANES), lambda i: (i, 0, 0)),
        out_shape=jax.ShapeDtypeStruct((steps, packed, LANES), BF16),
        scratch_shapes=[pltpu.VMEM((height, n_sp * LANES), BF16)] if n_sp else [],
    )(field, sibling, kron, *([spectrum, table] if n_sp else []))


def own_map(field, sibling, kron, start, steps, cost=0):
    chans = field.shape[0]
    outs = kron.shape[0] // ROWS
    depth = chans * ROWS

    def kernel(a_ref, b_ref, w_ref, out):
        def product(cols, width):
            a = a_ref[:, :, cols].reshape(depth, width)
            b = b_ref[:, :, cols].reshape(depth, width)
            acc = jnp.dot(w_ref[:, :depth], a, preferred_element_type=F32) + jnp.dot(
                w_ref[:, depth:], b, preferred_element_type=F32
            )
            out[:, :, cols] = acc.reshape(outs, ROWS, width)

        @pl.loop(0, FULL)
        def _(n):
            product(pl.ds(pl.multiple_of(n * WIDE, WIDE), WIDE), WIDE)

        product(slice(FULL * WIDE, LON), REST)

    rows = pl.BlockSpec((chans, ROWS, LON), lambda i: (0, start + i, 0))
    return call(
        kernel,
        "own_map",
        cost,
        grid=(steps,),
        in_specs=[rows, rows, const_spec(kron.shape)],
        out_specs=pl.BlockSpec((outs, ROWS, LON), lambda i: (0, i, 0)),
        out_shape=jax.ShapeDtypeStruct((outs, steps * ROWS, LON), F32),
    )(field, sibling, kron)


def gelu(v):
    return 0.5 * v * (1.0 + lax.erf(v * math.sqrt(0.5)))


def finish(previous, own, spectrum, table, received, start, steps, own_start, shape):
    outs = own.shape[0]
    height = outs * ROWS
    group = LANES // TAIL
    heights = [got.shape[1] * LANES // LON for got, _ in received]
    n_sp = spectrum[0].shape[0]
    sizes = [part.shape[1] for part in spectrum]

    def kernel(*refs):
        refs = refs[1:] if previous is not None else refs
        o_ref, t_ref = refs[:2]
        packs, lats = refs[2 : 2 + len(received)], refs[2 + len(received) : -2]
        out, lat = refs[-2], refs[-1]
        at = 0
        for ref, per in zip(lats, sizes):
            for k in range(n_sp):
                lat[at : at + per * ROWS, k * LANES : (k + 1) * LANES] = ref[k].reshape(
                    per * ROWS, LANES
                )
            at += per * ROWS

        def product(cols, width):
            spectral = jnp.dot(lat[...], t_ref[:, cols], preferred_element_type=F32)
            return spectral * (1.0 / LON) + o_ref[:, :, cols].reshape(height, width)

        @pl.loop(0, FULL)
        def _(n):
            cols = pl.ds(pl.multiple_of(n * WIDE, WIDE), WIDE)
            acc = product(cols, WIDE)
            far = []
            for p_ref, high in zip(packs, heights):
                base = pl.multiple_of(n * 2 * high, 2 * high)
                far.append([p_ref[0, pl.ds(base + i * high, high), :] for i in range(2)])
            far = jnp.concatenate([jnp.concatenate(pair, axis=1) for pair in far], axis=0)
            value = gelu(acc + far.astype(F32)).astype(BF16)
            out[:, :, cols] = value.reshape(outs, ROWS, WIDE)

        acc = product(slice(FULL * WIDE, LON), REST)
        far, tail = [], []
        for p_ref, high in zip(packs, heights):
            far.append(p_ref[0, FULL * 2 * high : (FULL * 2 + 1) * high, :])
            tails = p_ref[0, (FULL * 2 + 1) * high :, :].astype(F32)
            tail += [tails[:, q * TAIL : (q + 1) * TAIL] for q in range(group)]
        far = jnp.concatenate(far, axis=0).astype(F32)
        tail = jnp.concatenate(tail, axis=0)
        one = gelu(acc[:, :LANES] + far).astype(BF16)
        out[:, :, FULL * WIDE : FULL * WIDE + LANES] = one.reshape(outs, ROWS, LANES)
        two = gelu(acc[:, LANES:] + tail).astype(BF16)
        out[:, :, FULL * WIDE + LANES :] = two.reshape(outs, ROWS, TAIL)

    operands = [own, table, *[got for got, _ in received], *spectrum]
    specs = [
        pl.BlockSpec((outs, ROWS, LON), lambda i: (0, own_start + i, 0)),
        const_spec(table.shape),
    ] + [
        pl.BlockSpec((1, got.shape[1], LANES), functools.partial(lambda first, i: (first + i, 0, 0), first))
        for got, first in received
    ] + [
        pl.BlockSpec((n_sp, per, ROWS, LANES), lambda i: (0, 0, start + i, 0)) for per in sizes
    ]
    aliases = {}
    if previous is not None:
        operands = [previous] + operands
        specs = [pl.BlockSpec(memory_space=pl.ANY)] + specs
        aliases = {0: 0}
    return call(
        kernel,
        "finish",
        grid=(steps,),
        in_specs=specs,
        out_specs=pl.BlockSpec((outs, ROWS, LON), lambda i: (0, start + i, 0)),
        out_shape=jax.ShapeDtypeStruct(shape, BF16),
        input_output_aliases=aliases,
        scratch_shapes=[pltpu.VMEM((height, n_sp * LANES), BF16)],
    )(*operands)


def after(value, *others):
    return lax.optimization_barrier((value, *others))[0]


def row_plan(total):
    unit = total // 12
    last = total - 11 * unit
    return [unit, unit, 3 * unit, 3 * unit, 3 * unit, last], [4 * unit, 4 * unit, 3 * unit, last]


def tiled_body(state_field, spectral_weight, mode_gain, bypass_weight):
    chans, rows, _ = state_field.shape
    modes = spectral_weight.shape[1]
    n_sp, n_ch = lax.axis_size("sp"), lax.axis_size("ch")
    ch = lax.axis_index("ch")
    near, far = jnp.bitwise_xor(ch, 1), jnp.bitwise_xor(ch, 2)

    def to_near(value):
        return lax.ppermute(value, "ch", [(i, i ^ 1) for i in range(n_ch)])

    def to_far(value):
        return lax.ppermute(value, "ch", [(i, i ^ 2) for i in range(n_ch)])

    def across(blocks):
        return lax.all_to_all(blocks, "sp", 0, 0)

    plan, carried_plan = row_plan(rows // ROWS)
    plain = chans - CARRY

    near_first = to_near(lax.slice_in_dim(state_field, 0, sum(plan[:2]) * ROWS, axis=1))

    def rows_of(index):
        return lax.dynamic_slice_in_dim(bypass_weight, index * chans, chans, 0)

    chip_rows = jnp.concatenate([rows_of(ch), rows_of(near)], axis=0)
    far_columns = lax.dynamic_slice_in_dim(chip_rows, far * chans, chans, 1)
    kron_far = kron_map(far_columns[:, :plain])
    near_field = to_near(after(state_field, near_first, kron_far))
    near_weight = to_near(after(spectral_weight, near_first))

    sent, received = [], []

    def partial_rows(*others):
        i = len(sent)
        sibling = near_field if i > 1 else near_first
        kron = after(kron_far, *others)
        sent.append(partial_map(state_field, sibling, kron, sum(plan[:i]), plan[i], MAP_COST[i]))

    def send_rows(*others):
        received.append(to_far(after(sent[len(received)], *others)))

    half = chans // 2
    table = lon_table(n_sp, modes, False)
    inverse = lon_table(n_sp, modes, True)
    lat = lat_table()
    gain = jnp.pad(mode_gain, ((0, 0), (0, KPAD - L))).reshape(chans, 1, KPAD)
    far_gain = to_far(gain)
    partial_rows()
    send_rows(far_gain)
    bands = [lon_forward(state_field, after(table, sent[0]), 0, half, n_sp)]
    partial_rows(bands[0])
    send_rows(far_gain)
    partial_rows(sent[1])
    send_rows(*received[:2])
    partial_rows(sent[2])
    send_rows(received[2])
    bands.append(lon_forward(state_field, after(table, sent[3]), half, half, n_sp))
    kron_own = kron_map(lax.dynamic_slice_in_dim(chip_rows, ch * chans, chans, 1))
    kron_carried = kron_map(far_columns[:, plain:])
    middle = sum(plan[:2])
    own = [own_map(state_field, near_field, after(kron_own, sent[3]), 0, middle)]
    bands[1] = after(bands[1], sent[3], own[0])
    weights = pick_weights(ch, spectral_weight, near_weight)
    carried_gain = after(far_gain, weights)[plain:]
    bands = [across(b) for b in bands]
    spectra = [lat_forward(bands[0], lat)]
    own.append(own_map(state_field, near_field, after(kron_own, spectra[0]), middle, sum(plan[2:]), OWN_COST))
    spectra.append(lat_forward(bands[1], after(lat, own[1], weights, kron_carried, carried_gain)))
    spectra = [s.reshape(2, modes, -1, KPAD) for s in spectra]
    near_spectra = [to_near(s) for s in spectra]

    parts = [plain - 16, 16]
    own_mixed, carried, sends = mix(weights, spectra + near_spectra, parts)
    far_mixed = [to_far(after(s, received[3])) for s in sends]
    carried = lat_backward(carried, None, carried_gain, lat, 0, CARRY, n_sp)
    carried = across(carried)

    back = [
        lat_backward(own_mixed, None, gain, lat, plain, CARRY, n_sp),
        lat_backward(own_mixed, far_mixed[0], gain, lat, 0, parts[0], n_sp),
        lat_backward(own_mixed, far_mixed[1], gain, lat, parts[0], parts[1], n_sp, LAT_COST),
    ]
    spectrum = []
    for b in back:
        spectrum.append(across(after(b, spectrum[-1] if spectrum else carried)))
    spectrum = spectrum[1:] + spectrum[:1]
    for _ in range(2):
        partial_rows(*sends)
        send_rows(far_mixed[1])

    kron_carried = after(kron_carried, back[2])
    late = []
    for i, steps in enumerate(carried_plan):
        at = sum(carried_plan[:i])
        block = partial_map(
            state_field, near_field, kron_carried, at, steps, CARRIED_COST[i], carried, inverse
        )
        late.append(to_far(after(block, late[0] if i > 1 else received[5 - i])))

    out = None
    cuts = sorted({sum(p[:i]) for p in (plan, carried_plan) for i in range(len(p) + 1)})
    for start, end in zip(cuts, cuts[1:]):
        got = []
        for blocks, p in ((received, plan), (late, carried_plan)):
            i = max(i for i in range(len(p)) if sum(p[:i]) <= start)
            got.append((blocks[i], start - sum(p[:i])))
        part = start >= middle
        out = finish(
            out, own[part], spectrum, inverse, got, start, end - start, start - part * middle,
            state_field.shape,
        )
    return out


def body(state_field, spectral_weight, mode_gain, bypass_weight):
    chans, rows, _ = state_field.shape
    modes = spectral_weight.shape[1]
    n_sp, n_ch = lax.axis_size("sp"), lax.axis_size("ch")
    whole_tiles = (
        n_ch == 4
        and 2 * modes == LANES
        and chans == 64
        and rows % (12 * ROWS) == 0
    )
    run = tiled_body if whole_tiles else plain_body
    return run(state_field, spectral_weight, mode_gain, bypass_weight)


def solution(mesh):
    in_specs = (P(("grp", "ch"), "sp", None), P(None, "sp", "ch", None), P("ch", None), P())
    out_specs = P(("grp", "ch"), "sp", None)
    return jax.shard_map(body, mesh=mesh, in_specs=in_specs, out_specs=out_specs, check_vma=False)
```

```python
import functools
import math

import jax
import jax.numpy as jnp
import ml_dtypes
import numpy as np
from jax import lax
from jax.experimental import pallas as pl
from jax.experimental.pallas import tpu as pltpu
from jax.sharding import PartitionSpec as P

LAT = 768
LON = 1440
M = 256
L = 320

LANES = 128
ROWS = 16
KPAD = 384
VMEM = 56 * 1024 * 1024
F32 = jnp.float32
BF16 = jnp.bfloat16


def make_tables():
    lon_index = jnp.arange(LON, dtype=jnp.int32)
    mode_index = jnp.arange(M, dtype=jnp.int32)
    phase_lon = jnp.mod(lon_index[:, None] * mode_index[None, :], LON).astype(jnp.float32) * (
        2.0 * math.pi / LON
    )
    fwd_lon = jnp.stack([jnp.cos(phase_lon), -jnp.sin(phase_lon)], axis=1).astype(jnp.bfloat16)
    mode_weight = jnp.where(mode_index == 0, 1.0, 2.0).astype(jnp.float32)
    inv_lon = jnp.stack(
        [mode_weight[:, None] * jnp.cos(phase_lon).T, -mode_weight[:, None] * jnp.sin(phase_lon).T],
        axis=0,
    ).astype(jnp.bfloat16)
    lat_index = jnp.arange(LAT, dtype=jnp.int32)
    wave_index = jnp.arange(L, dtype=jnp.int32)
    wave_number = jnp.where(wave_index < L // 2, wave_index, wave_index - L)
    phase_lat = jnp.mod(lat_index[:, None] * wave_number[None, :], LAT).astype(jnp.float32) * (
        2.0 * math.pi / LAT
    )
    fwd_lat = jnp.stack([jnp.cos(phase_lat), jnp.sin(phase_lat)], axis=1).astype(jnp.bfloat16)
    inv_lat = jnp.stack([jnp.cos(phase_lat).T, jnp.sin(phase_lat).T], axis=1).astype(jnp.bfloat16)
    return (fwd_lon, inv_lon, fwd_lat, inv_lat)


def mix_modes(weights, inputs):
    out_real = jnp.einsum(
        "mcd,cmk->dmk", weights[0], inputs[:, 0], preferred_element_type=jnp.float32
    ) - jnp.einsum("mcd,cmk->dmk", weights[1], inputs[:, 1], preferred_element_type=jnp.float32)
    out_imag = jnp.einsum(
        "mcd,cmk->dmk", weights[1], inputs[:, 0], preferred_element_type=jnp.float32
    ) + jnp.einsum("mcd,cmk->dmk", weights[0], inputs[:, 1], preferred_element_type=jnp.float32)
    return jnp.stack([out_real, out_imag], axis=1)


def plain_body(state_field, spectral_weight, mode_gain, bypass_weight):
    fwd_lon, inv_lon, fwd_lat, inv_lat = make_tables()
    chan_count = state_field.shape[0]
    band_rows = state_field.shape[1]
    flat_field = state_field.reshape(chan_count * band_rows, LON)
    lon_spectrum = (
        jnp.dot(flat_field, fwd_lon.reshape(LON, 2 * M), preferred_element_type=jnp.float32)
        .astype(jnp.bfloat16)
        .reshape(chan_count, band_rows, 2, M)
    )
    all_latitudes = lax.all_to_all(lon_spectrum, "sp", split_axis=3, concat_axis=1, tiled=True)
    lat_parts = jnp.einsum(
        "clrm,lsk->crmsk", all_latitudes, fwd_lat, preferred_element_type=jnp.float32
    )
    real_part = lat_parts[:, 0, :, 0] + lat_parts[:, 1, :, 1]
    imag_part = lat_parts[:, 1, :, 0] - lat_parts[:, 0, :, 1]
    modes_in = jnp.stack([real_part, imag_part], axis=1).astype(jnp.bfloat16)
    weight_rows = lax.all_to_all(spectral_weight, "ch", split_axis=3, concat_axis=2, tiled=True)
    all_inputs = lax.all_gather(modes_in, "ch", axis=0, tiled=True)
    mixed = mix_modes(weight_rows, all_inputs)
    scaled = (mixed * mode_gain[:, None, None, :]).astype(jnp.bfloat16)
    back_parts = jnp.einsum("drmk,ksl->drmsl", scaled, inv_lat, preferred_element_type=jnp.float32)
    back_real = back_parts[:, 0, :, 0] - back_parts[:, 1, :, 1]
    back_imag = back_parts[:, 0, :, 1] + back_parts[:, 1, :, 0]
    lat_field = (jnp.stack([back_real, back_imag], axis=1) * (1.0 / LAT)).astype(jnp.bfloat16)
    band_spectrum = lax.all_to_all(lat_field, "sp", split_axis=3, concat_axis=2, tiled=True)
    spectral_out = jnp.einsum(
        "drml,rmx->dlx", band_spectrum, inv_lon, preferred_element_type=jnp.float32
    ) * (1.0 / LON)
    out_width = bypass_weight.shape[1] // lax.axis_size("ch")
    own_columns = lax.dynamic_slice_in_dim(
        bypass_weight, lax.axis_index("ch") * out_width, out_width, 1
    )
    bypass = jnp.einsum(
        "cd,clx->dlx",
        own_columns,
        lax.all_gather(state_field, "ch", axis=0, tiled=True),
        preferred_element_type=jnp.float32,
    ).astype(jnp.bfloat16)
    return jax.nn.gelu(spectral_out + bypass.astype(jnp.float32), approximate=False).astype(
        jnp.bfloat16
    )


def lon_table(n_sp, modes, transposed):
    col = np.arange(n_sp * 2 * modes)
    imag, mode = (col // modes) % 2, col // (2 * modes) * modes + col % modes
    angle = (np.arange(LON)[:, None] * mode[None, :]) % LON * (2.0 * math.pi / LON)
    value = np.where(imag == 0, np.cos(angle), -np.sin(angle))
    if transposed:
        value = (value * np.where(mode == 0, 1.0, 2.0)).T
    return jnp.asarray(value.astype(ml_dtypes.bfloat16))


def lat_table():
    k = np.arange(L)
    kappa = np.where(k < L // 2, k, k - L)
    angle = (np.arange(LAT)[:, None] * kappa[None, :]) % LAT * (2.0 * math.pi / LAT)
    value = np.zeros((LAT, 2, KPAD))
    value[:, 0, :L], value[:, 1, :L] = np.cos(angle), np.sin(angle)
    return jnp.asarray(value.reshape(LAT, 2 * KPAD).astype(ml_dtypes.bfloat16))


MAP_COST = [0, 0, 0, 120, 0, 0]
CARRIED_COST = [120, 120, 40, 40]
CARRY = 20
LAT_COST = 150
OWN_COST = 50


def call(kernel, name, cost=0, **kwargs):
    return pl.pallas_call(
        kernel,
        name=name,
        compiler_params=pltpu.CompilerParams(vmem_limit_bytes=VMEM),
        cost_estimate=pl.CostEstimate(
            flops=1 + int(cost * 1e9), bytes_accessed=1, transcendentals=0
        ),
        **kwargs,
    )


def const_spec(shape):
    return pl.BlockSpec(shape, lambda *_: (0,) * len(shape))


def kron_map(weight):
    c, d = weight.shape
    high, wide = d * ROWS, c * ROWS

    def kernel(w_ref, out):
        iota = functools.partial(lax.broadcasted_iota, jnp.int32)
        left = (iota((high, d), 0) // ROWS == iota((high, d), 1)).astype(F32).astype(BF16)
        right = (iota((c, wide), 1) // ROWS == iota((c, wide), 0)).astype(F32).astype(BF16)
        tall = lax.dot_general(
            left, w_ref[...], (((1,), (1,)), ((), ())), preferred_element_type=F32
        ).astype(BF16)
        value = jnp.dot(tall, right, preferred_element_type=F32)
        same = iota((high, wide), 0) % ROWS == iota((high, wide), 1) % ROWS
        out[...] = jnp.where(same, value, 0.0).astype(BF16)

    return call(
        kernel, "kron_map", out_shape=jax.ShapeDtypeStruct((high, wide), BF16)
    )(weight)


def pick_weights(ch, own, sibling):
    _, modes, chans, _ = own.shape
    half = LANES // 2
    step = modes // 4

    def kernel(ch_ref, a0, a1, b0, b1, out):
        for parity in range(2):

            @pl.when(ch_ref[0] % 2 == parity)
            def _():
                cols = slice(parity * half, (parity + 1) * half)
                for i, pair in enumerate(((a0, a1), (b0, b1))):
                    out[:, :, i * chans : (i + 1) * chans, :] = jnp.concatenate(
                        [ref[:, :, :, cols] for ref in pair], axis=-1
                    )

    def tile(far):
        return pl.BlockSpec(
            (2, step, chans, LANES), lambda i, ch_ref: (0, i, 0, (ch_ref[0] // 2 + far) % 2)
        )

    return call(
        kernel,
        "pick_weights",
        grid_spec=pltpu.PrefetchScalarGridSpec(
            num_scalar_prefetch=1,
            grid=(modes // step,),
            in_specs=[tile(0), tile(1), tile(0), tile(1)],
            out_specs=pl.BlockSpec((2, step, 2 * chans, LANES), lambda i, ch_ref: (0, i, 0, 0)),
        ),
        out_shape=jax.ShapeDtypeStruct((2, modes, 2 * chans, LANES), BF16),
    )(ch.reshape(1), own, own, sibling, sibling)


def lon_forward(field, table, start, count, n_sp):
    rows = field.shape[1]
    step = 4

    def kernel(s_ref, t_ref, out):
        s = s_ref[...].reshape(step * rows, LON)
        acc = jnp.dot(s, t_ref[...], preferred_element_type=F32)
        for k in range(n_sp):
            part = acc[:, k * LANES : (k + 1) * LANES].astype(BF16)
            out[k] = part.reshape(step, rows, LANES)

    return call(
        kernel,
        "lon_forward",
        grid=(count // step,),
        in_specs=[
            pl.BlockSpec((step, rows, LON), lambda i: (start // step + i, 0, 0)),
            const_spec(table.shape),
        ],
        out_specs=pl.BlockSpec((n_sp, step, rows, LANES), lambda i: (0, i, 0, 0)),
        out_shape=jax.ShapeDtypeStruct((n_sp, count, rows, LANES), BF16),
    )(field, table)


def lat_forward(bands, table):
    n_sp, count, rows, _ = bands.shape
    step = ROWS
    half = LANES // 2

    def kernel(x_ref, t_ref, out, left, right):
        for c in range(step):
            x = x_ref[:, c].reshape(n_sp * rows, LANES)
            left[c * LANES : (c + 1) * LANES, :] = x.T
        for c in range(step):
            g = jnp.dot(
                left[c * LANES : (c + 1) * LANES, :], t_ref[...], preferred_element_type=F32
            )
            right[c, :half, :] = g[:half, :KPAD] + g[half:, KPAD:]
            right[c, half:, :] = g[half:, :KPAD] - g[:half, KPAD:]
        out[...] = jnp.transpose(right[...], (1, 0, 2)).astype(BF16)

    return call(
        kernel,
        "lat_forward",
        grid=(count // step,),
        in_specs=[
            pl.BlockSpec((n_sp, step, rows, LANES), lambda i: (0, i, 0, 0)),
            const_spec(table.shape),
        ],
        out_specs=pl.BlockSpec((LANES, step, KPAD), lambda i: (0, i, 0)),
        out_shape=jax.ShapeDtypeStruct((LANES, count, KPAD), BF16),
        scratch_shapes=[
            pltpu.VMEM((step * LANES, n_sp * rows), BF16),
            pltpu.VMEM((step, LANES, KPAD), F32),
        ],
    )(bands, table)


def mix(weights, spectra, parts):
    modes, chans, outs2 = weights.shape[1:]
    outs = outs2 // 2
    step = ROWS
    n_in = len(spectra)
    carry = outs - sum(parts)

    def kernel(w_ref, *refs):
        ins, own, carried, sends = refs[:n_in], refs[n_in], refs[n_in + 1], refs[n_in + 2 : -1]
        scratch = refs[-1]
        for m in range(step):
            y = jnp.concatenate([ref[r, m] for r in range(2) for ref in ins], axis=0)
            wr, wi = w_ref[0, m], w_ref[1, m]
            w = jnp.concatenate(
                [jnp.concatenate([wr, wi], axis=1), jnp.concatenate([-wi, wr], axis=1)], axis=0
            )
            scratch[m] = lax.dot_general(
                w, y, (((0,), (0,)), ((), ())), preferred_element_type=F32
            )
        for r in range(2):
            base = r * outs2
            own[r] = jnp.transpose(scratch[:, base : base + outs, :], (1, 0, 2))
        far = [
            jnp.transpose(scratch[:, r * outs2 + outs : (r + 1) * outs2, :], (1, 0, 2))
            for r in range(2)
        ]
        for r in range(2):
            carried[r] = far[r][outs - carry :]
        for i, send in enumerate(sends):
            block = [f[sum(parts[:i]) : sum(parts[: i + 1])] for f in far]
            for r in range(2):
                for t in range(2):
                    send[2 * r + t] = block[r][:, :, t * LANES : (t + 1) * LANES].astype(BF16)
            tail = [b[:, :, 2 * LANES : 2 * LANES + LANES // 2] for b in block]
            send[4] = jnp.concatenate(tail, axis=-1).astype(BF16)

    res = call(
        kernel,
        "mix",
        grid=(modes // step,),
        in_specs=[pl.BlockSpec((2, step, chans, outs2), lambda i: (0, i, 0, 0))]
        + [pl.BlockSpec((2, step, s.shape[2], KPAD), lambda i: (0, i, 0, 0)) for s in spectra],
        out_specs=[pl.BlockSpec((2, n, step, KPAD), lambda i: (0, 0, i, 0)) for n in (outs, carry)]
        + [pl.BlockSpec((5, per, step, LANES), lambda i: (0, 0, i, 0)) for per in parts],
        out_shape=[jax.ShapeDtypeStruct((2, n, modes, KPAD), F32) for n in (outs, carry)]
        + [jax.ShapeDtypeStruct((5, per, modes, LANES), BF16) for per in parts],
        scratch_shapes=[pltpu.VMEM((step, 2 * outs2, KPAD), F32)],
    )(weights, *spectra)
    return res[0], res[1], res[2:]


def lat_backward(own, far, gain, table, start, per, n_sp, cost=0):
    modes = own.shape[2]
    rows = LAT // n_sp
    step = 4

    def kernel(own_ref, *refs):
        far_ref = refs[0] if far is not None else None
        g_ref, t_ref, result = refs[-3:]
        for pair in range(step // 2):
            blocks = []
            for d in (2 * pair, 2 * pair + 1):
                z = []
                for r in range(2):
                    if far_ref is None:
                        z.append((own_ref[r, d] * g_ref[d]).astype(BF16))
                        continue
                    tail = far_ref[4, d][:, r * (LANES // 2) : (r + 1) * (LANES // 2)]
                    sent = jnp.concatenate(
                        [
                            far_ref[2 * r, d].astype(F32),
                            far_ref[2 * r + 1, d].astype(F32),
                            tail.astype(F32),
                            jnp.zeros((modes, LANES // 2), F32),
                        ],
                        axis=-1,
                    )
                    z.append(((own_ref[r, d] + sent) * g_ref[d]).astype(BF16))
                blocks.append(jnp.concatenate([z[0], -z[1]], axis=1))
                blocks.append(jnp.concatenate([z[1], z[0]], axis=1))
            both = jnp.concatenate(blocks, axis=0)
            out = lax.dot_general(
                t_ref[...], both, (((1,), (1,)), ((), ())), preferred_element_type=F32
            ) * (1.0 / LAT)
            for k in range(n_sp):
                for i in range(2):
                    result[k, 2 * pair + i] = out[
                        k * rows : (k + 1) * rows, i * LANES : (i + 1) * LANES
                    ].astype(BF16)

    return call(
        kernel,
        "lat_backward",
        cost,
        grid=(per // step,),
        in_specs=[
            pl.BlockSpec((2, step, modes, KPAD), lambda i: (0, start // step + i, 0, 0)),
        ]
        + [pl.BlockSpec((5, step, modes, LANES), lambda i: (0, i, 0, 0))] * (far is not None)
        + [
            pl.BlockSpec((step, 1, KPAD), lambda i: (start // step + i, 0, 0)),
            const_spec(table.shape),
        ],
        out_specs=pl.BlockSpec((n_sp, step, rows, LANES), lambda i: (0, i, 0, 0)),
        out_shape=jax.ShapeDtypeStruct((n_sp, per, rows, LANES), BF16),
    )(*([own] if far is None else [own, far]), gain, table)


WIDE = 2 * LANES
FULL = LON // WIDE
REST = LON - FULL * WIDE
TAIL = REST - LANES


def partial_map(field, sibling, kron, start, steps, cost, spectrum=None, table=None):
    chans = field.shape[0]
    outs = kron.shape[0] // ROWS
    height = outs * ROWS
    depth = chans * ROWS
    packed = height * LON // LANES
    group = LANES // TAIL

    n_sp = spectrum.shape[0] if spectrum is not None else 0

    def kernel(a_ref, b_ref, w_ref, *refs):
        out = refs[2] if n_sp else refs[0]
        if n_sp:
            s_ref, t_ref, _, lat = refs
            for k in range(n_sp):
                lat[:, k * LANES : (k + 1) * LANES] = s_ref[k].reshape(height, LANES)

        def product(cols, width):
            a = a_ref[:, :, cols].reshape(depth, width)
            b = b_ref[:, :, cols].reshape(depth, width)
            acc = jnp.dot(w_ref[:, :depth], a, preferred_element_type=F32) + jnp.dot(
                w_ref[:, depth:], b, preferred_element_type=F32
            )
            if n_sp:
                spectral = jnp.dot(lat[...], t_ref[:, cols], preferred_element_type=F32)
                acc = acc + spectral * (1.0 / LON)
            return acc

        @pl.loop(0, FULL)
        def _(n):
            acc = product(pl.ds(pl.multiple_of(n * WIDE, WIDE), WIDE), WIDE).astype(BF16)
            base = pl.multiple_of(n * 2 * height, 2 * height)
            out[0, pl.ds(base, height), :] = acc[:, :LANES]
            out[0, pl.ds(base + height, height), :] = acc[:, LANES:]

        acc = product(slice(FULL * WIDE, LON), REST)
        out[0, FULL * 2 * height : (FULL * 2 + 1) * height, :] = acc[:, :LANES].astype(BF16)
        tail = acc[:, LANES:]
        size = height // group
        out[0, (FULL * 2 + 1) * height :, :] = jnp.concatenate(
            [tail[q * size : (q + 1) * size] for q in range(group)], axis=1
        ).astype(BF16)

    return call(
        kernel,
        "partial_map",
        cost,
        grid=(steps,),
        in_specs=[
            pl.BlockSpec((chans, ROWS, LON), lambda i: (0, start + i, 0)),
            pl.BlockSpec((chans, ROWS, LON), lambda i: (0, start + i, 0)),
            const_spec(kron.shape),
        ]
        + (
            [
                pl.BlockSpec((n_sp, outs, ROWS, LANES), lambda i: (0, 0, start + i, 0)),
                const_spec(table.shape),
            ]
            if n_sp
            else []
        ),
        out_specs=pl.BlockSpec((1, packed, LANES), lambda i: (i, 0, 0)),
        out_shape=jax.ShapeDtypeStruct((steps, packed, LANES), BF16),
        scratch_shapes=[pltpu.VMEM((height, n_sp * LANES), BF16)] if n_sp else [],
    )(field, sibling, kron, *([spectrum, table] if n_sp else []))


def own_map(field, sibling, kron, start, steps, cost=0):
    chans = field.shape[0]
    outs = kron.shape[0] // ROWS
    depth = chans * ROWS

    def kernel(a_ref, b_ref, w_ref, out):
        def product(cols, width):
            a = a_ref[:, :, cols].reshape(depth, width)
            b = b_ref[:, :, cols].reshape(depth, width)
            acc = jnp.dot(w_ref[:, :depth], a, preferred_element_type=F32) + jnp.dot(
                w_ref[:, depth:], b, preferred_element_type=F32
            )
            out[:, :, cols] = acc.reshape(outs, ROWS, width)

        @pl.loop(0, FULL)
        def _(n):
            product(pl.ds(pl.multiple_of(n * WIDE, WIDE), WIDE), WIDE)

        product(slice(FULL * WIDE, LON), REST)

    rows = pl.BlockSpec((chans, ROWS, LON), lambda i: (0, start + i, 0))
    return call(
        kernel,
        "own_map",
        cost,
        grid=(steps,),
        in_specs=[rows, rows, const_spec(kron.shape)],
        out_specs=pl.BlockSpec((outs, ROWS, LON), lambda i: (0, i, 0)),
        out_shape=jax.ShapeDtypeStruct((outs, steps * ROWS, LON), F32),
    )(field, sibling, kron)


def gelu(v):
    return 0.5 * v * (1.0 + lax.erf(v * math.sqrt(0.5)))


def finish(previous, own, spectrum, table, received, start, steps, own_start, shape):
    outs = own.shape[0]
    height = outs * ROWS
    group = LANES // TAIL
    heights = [got.shape[1] * LANES // LON for got, _ in received]
    n_sp = spectrum[0].shape[0]
    sizes = [part.shape[1] for part in spectrum]

    def kernel(*refs):
        refs = refs[1:] if previous is not None else refs
        o_ref, t_ref = refs[:2]
        packs, lats = refs[2 : 2 + len(received)], refs[2 + len(received) : -2]
        out, lat = refs[-2], refs[-1]
        at = 0
        for ref, per in zip(lats, sizes):
            for k in range(n_sp):
                lat[at : at + per * ROWS, k * LANES : (k + 1) * LANES] = ref[k].reshape(
                    per * ROWS, LANES
                )
            at += per * ROWS

        def product(cols, width):
            spectral = jnp.dot(lat[...], t_ref[:, cols], preferred_element_type=F32)
            return spectral * (1.0 / LON) + o_ref[:, :, cols].reshape(height, width)

        @pl.loop(0, FULL)
        def _(n):
            cols = pl.ds(pl.multiple_of(n * WIDE, WIDE), WIDE)
            acc = product(cols, WIDE)
            far = []
            for p_ref, high in zip(packs, heights):
                base = pl.multiple_of(n * 2 * high, 2 * high)
                far.append([p_ref[0, pl.ds(base + i * high, high), :] for i in range(2)])
            far = jnp.concatenate([jnp.concatenate(pair, axis=1) for pair in far], axis=0)
            value = gelu(acc + far.astype(F32)).astype(BF16)
            out[:, :, cols] = value.reshape(outs, ROWS, WIDE)

        acc = product(slice(FULL * WIDE, LON), REST)
        far, tail = [], []
        for p_ref, high in zip(packs, heights):
            far.append(p_ref[0, FULL * 2 * high : (FULL * 2 + 1) * high, :])
            tails = p_ref[0, (FULL * 2 + 1) * high :, :].astype(F32)
            tail += [tails[:, q * TAIL : (q + 1) * TAIL] for q in range(group)]
        far = jnp.concatenate(far, axis=0).astype(F32)
        tail = jnp.concatenate(tail, axis=0)
        one = gelu(acc[:, :LANES] + far).astype(BF16)
        out[:, :, FULL * WIDE : FULL * WIDE + LANES] = one.reshape(outs, ROWS, LANES)
        two = gelu(acc[:, LANES:] + tail).astype(BF16)
        out[:, :, FULL * WIDE + LANES :] = two.reshape(outs, ROWS, TAIL)

    operands = [own, table, *[got for got, _ in received], *spectrum]
    specs = [
        pl.BlockSpec((outs, ROWS, LON), lambda i: (0, own_start + i, 0)),
        const_spec(table.shape),
    ] + [
        pl.BlockSpec((1, got.shape[1], LANES), functools.partial(lambda first, i: (first + i, 0, 0), first))
        for got, first in received
    ] + [
        pl.BlockSpec((n_sp, per, ROWS, LANES), lambda i: (0, 0, start + i, 0)) for per in sizes
    ]
    aliases = {}
    if previous is not None:
        operands = [previous] + operands
        specs = [pl.BlockSpec(memory_space=pl.ANY)] + specs
        aliases = {0: 0}
    return call(
        kernel,
        "finish",
        grid=(steps,),
        in_specs=specs,
        out_specs=pl.BlockSpec((outs, ROWS, LON), lambda i: (0, start + i, 0)),
        out_shape=jax.ShapeDtypeStruct(shape, BF16),
        input_output_aliases=aliases,
        scratch_shapes=[pltpu.VMEM((height, n_sp * LANES), BF16)],
    )(*operands)


def after(value, *others):
    return lax.optimization_barrier((value, *others))[0]


def row_plan(total):
    unit = total // 12
    last = total - 11 * unit
    return [unit, unit, 3 * unit, 3 * unit, 3 * unit, last], [4 * unit, 4 * unit, 3 * unit, last]


def tiled_body(state_field, spectral_weight, mode_gain, bypass_weight):
    chans, rows, _ = state_field.shape
    modes = spectral_weight.shape[1]
    n_sp, n_ch = lax.axis_size("sp"), lax.axis_size("ch")
    ch = lax.axis_index("ch")
    near, far = jnp.bitwise_xor(ch, 1), jnp.bitwise_xor(ch, 2)

    def to_near(value):
        return lax.ppermute(value, "ch", [(i, i ^ 1) for i in range(n_ch)])

    def to_far(value):
        return lax.ppermute(value, "ch", [(i, i ^ 2) for i in range(n_ch)])

    def across(blocks):
        return lax.all_to_all(blocks, "sp", 0, 0)

    plan, carried_plan = row_plan(rows // ROWS)
    plain = chans - CARRY

    near_first = to_near(lax.slice_in_dim(state_field, 0, sum(plan[:2]) * ROWS, axis=1))

    def rows_of(index):
        return lax.dynamic_slice_in_dim(bypass_weight, index * chans, chans, 0)

    chip_rows = jnp.concatenate([rows_of(ch), rows_of(near)], axis=0)
    far_columns = lax.dynamic_slice_in_dim(chip_rows, far * chans, chans, 1)
    kron_far = kron_map(far_columns[:, :plain])
    near_field = to_near(after(state_field, near_first, kron_far))
    near_weight = to_near(after(spectral_weight, near_first))

    sent, received = [], []

    def partial_rows(*others):
        i = len(sent)
        sibling = near_field if i > 1 else near_first
        kron = after(kron_far, *others)
        sent.append(partial_map(state_field, sibling, kron, sum(plan[:i]), plan[i], MAP_COST[i]))

    def send_rows(*others):
        received.append(to_far(after(sent[len(received)], *others)))

    half = chans // 2
    table = lon_table(n_sp, modes, False)
    inverse = lon_table(n_sp, modes, True)
    lat = lat_table()
    gain = jnp.pad(mode_gain, ((0, 0), (0, KPAD - L))).reshape(chans, 1, KPAD)
    far_gain = to_far(gain)
    partial_rows()
    send_rows(far_gain)
    bands = [lon_forward(state_field, after(table, sent[0]), 0, half, n_sp)]
    partial_rows(bands[0])
    send_rows(far_gain)
    partial_rows(sent[1])
    send_rows(*received[:2])
    partial_rows(sent[2])
    send_rows(received[2])
    bands.append(lon_forward(state_field, after(table, sent[3]), half, half, n_sp))
    own_columns = lax.dynamic_slice_in_dim(chip_rows, ch * chans, chans, 1)
    kron_own = kron_map(after(own_columns, sent[3]))
    kron_carried = kron_map(far_columns[:, plain:])
    middle = sum(plan[:2])
    own = [own_map(state_field, near_field, after(kron_own, sent[3]), 0, middle)]
    bands[1] = after(bands[1], sent[3], own[0])
    weights = pick_weights(ch, spectral_weight, near_weight)
    carried_gain = after(far_gain, weights)[plain:]
    bands = [across(b) for b in bands]
    spectra = [lat_forward(bands[0], lat)]
    own.append(own_map(state_field, near_field, after(kron_own, spectra[0]), middle, sum(plan[2:]), OWN_COST))
    spectra.append(lat_forward(bands[1], after(lat, own[1], weights, kron_carried, carried_gain)))
    spectra = [s.reshape(2, modes, -1, KPAD) for s in spectra]
    near_spectra = [to_near(s) for s in spectra]

    parts = [plain - 16, 16]
    own_mixed, carried, sends = mix(weights, spectra + near_spectra, parts)
    far_mixed = [to_far(after(s, received[3])) for s in sends]
    carried = lat_backward(carried, None, carried_gain, lat, 0, CARRY, n_sp)
    carried = across(carried)

    back = [
        lat_backward(own_mixed, None, gain, lat, plain, CARRY, n_sp),
        lat_backward(own_mixed, far_mixed[0], gain, lat, 0, parts[0], n_sp),
        lat_backward(own_mixed, far_mixed[1], gain, lat, parts[0], parts[1], n_sp, LAT_COST),
    ]
    spectrum = []
    for b in back:
        spectrum.append(across(after(b, spectrum[-1] if spectrum else carried)))
    spectrum = spectrum[1:] + spectrum[:1]
    for _ in range(2):
        partial_rows(*sends)
        send_rows(far_mixed[1])

    kron_carried = after(kron_carried, back[2])
    late = []
    for i, steps in enumerate(carried_plan):
        at = sum(carried_plan[:i])
        block = partial_map(
            state_field, near_field, kron_carried, at, steps, CARRIED_COST[i], carried, inverse
        )
        late.append(to_far(after(block, late[0] if i > 1 else received[5 - i])))

    out = None
    cuts = sorted({sum(p[:i]) for p in (plan, carried_plan) for i in range(len(p) + 1)})
    for start, end in zip(cuts, cuts[1:]):
        got = []
        for blocks, p in ((received, plan), (late, carried_plan)):
            i = max(i for i in range(len(p)) if sum(p[:i]) <= start)
            got.append((blocks[i], start - sum(p[:i])))
        part = start >= middle
        out = finish(
            out, own[part], spectrum, inverse, got, start, end - start, start - part * middle,
            state_field.shape,
        )
    return out


def body(state_field, spectral_weight, mode_gain, bypass_weight):
    chans, rows, _ = state_field.shape
    modes = spectral_weight.shape[1]
    n_sp, n_ch = lax.axis_size("sp"), lax.axis_size("ch")
    whole_tiles = (
        n_ch == 4
        and 2 * modes == LANES
        and chans == 64
        and rows % (12 * ROWS) == 0
    )
    run = tiled_body if whole_tiles else plain_body
    return run(state_field, spectral_weight, mode_gain, bypass_weight)


def solution(mesh):
    in_specs = (P(("grp", "ch"), "sp", None), P(None, "sp", "ch", None), P("ch", None), P())
    out_specs = P(("grp", "ch"), "sp", None)
    return jax.shard_map(body, mesh=mesh, in_specs=in_specs, out_specs=out_specs, check_vma=False)
```
